128 devices in a mesh: attn: 4 (over y), ffn: 32 (over x, z, core).
Axes of the slice: x: 4, y: 4, z: 4, core: 2. Of those that a mesh axis runs over, the one named last changes fastest.
Arguments:
- tokens: bfloat16 [1024, 7168], P(('attn', 'ffn')), may hold values from -6 to 6
- expert_ids: int32 [1024, 3], P(('attn', 'ffn')), may hold values from 0 to 15, all different within a row; in each aligned block of 8 rows (0 to 7, 8 to 15, ...) at most 3 rows name the same one
- gate_values: float32 [1024, 3], P(('attn', 'ffn')), may hold values from 0.2 to 1.5
- shared_gate: bfloat16 [7168, 5120], P(None, 'ffn'), may hold values from -0.0625 to 0.0625
- shared_up: bfloat16 [7168, 5120], P(None, 'ffn'), may hold values from -0.0625 to 0.0625
- shared_down: bfloat16 [5120, 7168], P('ffn'), may hold values from -0.078125 to 0.078125
- routed_gate: bfloat16 [32, 7168, 1280], P('ffn', None, 'attn'), may hold values from -0.0625 to 0.0625
- routed_up: bfloat16 [32, 7168, 1280], P('ffn', None, 'attn'), may hold values from -0.0625 to 0.0625
- routed_down: bfloat16 [32, 1280, 7168], P('ffn', 'attn'), may hold values from -0.125 to 0.125
Outputs:
- ffn_out: bfloat16 [1024, 7168], P(('attn', 'ffn'))
The draws below stay inside these ranges and needn't reach their ends.
Inputs may be any that keep to these rules, and one draw needn't show every extreme that they name: `expert_ids`: the three experts of a token differ; among the tokens of one device no expert is named more than 3 times, and that count is reached.
All inputs are finite; a program needn't handle non-finite values.
Results may differ from the reference program's by a relative error of at most 0.0055.
Values may be sent and summed in bfloat16 or wider, within the bound.
A program may use at most 128 MiB of HBM per device.

```python
import math
import jax
import jax.numpy as jnp
import numpy as np
from jax import lax

D = 7168
FF_WIN = 2560
FS = 5120
TOK_DEV = 8
FF_HALF = 1280
EXPERTS = 16
CAP = 3
TOKENS = 1024
N_ATTN = 4
N_FFN = 32


def block_levels(rng, shape, cuts, least, high):
    loudness = 1.0
    for dim, parts in cuts:
        steps = jax.random.uniform(jax.random.fold_in(jax.random.fold_in(rng, 6), dim), (parts,), jnp.float32, least / len(cuts), high / len(cuts))
        loudness = loudness * jnp.repeat(jnp.exp(steps), shape[dim] // parts).reshape((-1,) + (1,) * (len(shape) - 1 - dim))
    return loudness


def assign_block(stream_key, own, number, rows, amount, top, bound, slope):
    ranking = jax.random.permutation(stream_key, amount)
    crowded, common = load_shares(amount, rows * top, bound, slope, True), load_shares(amount, rows * top, bound, slope, False)
    places = jnp.arange(amount)

    def named(tallies, offset_by):
        used = int((tallies > 0).sum())
        fixed = max(1, used // 4)
        shifted = fixed + (places - fixed + offset_by * (used - fixed)) % max(1, amount - fixed)
        return jnp.zeros((amount,), jnp.int32).at[ranking[jnp.where(places < fixed, places, shifted)]].set(jnp.asarray(tallies, jnp.int32))

    tallies = jnp.where(number % 4 == 0, named(crowded, number // 4), named(common, number - number // 4 - 1))
    mixed = jax.random.permutation(jax.random.fold_in(own, 3), amount)
    source_of, sink = mixed[0:amount // 2 * 2:2], mixed[1:amount // 2 * 2:2]
    margin = jnp.minimum(tallies[source_of] - 1, bound - tallies[sink]) // 2
    margin = jnp.where((source_of == ranking[0]) | (sink == ranking[0]) | (tallies[sink] == 0), 0, jnp.maximum(margin, 0))
    shifted = jax.random.randint(jax.random.fold_in(own, 4), (amount // 2,), 0, 1 << 20) % (margin + 1)
    tallies = tallies.at[source_of].add(-shifted).at[sink].add(shifted)
    labels = jnp.searchsorted(jnp.cumsum(tallies), jnp.arange(rows * top), side="right").astype(jnp.int32)
    grid = labels.reshape(top, rows).T
    grid = grid[jax.random.permutation(jax.random.fold_in(own, 1), rows)]
    offset_by = jax.random.randint(jax.random.fold_in(own, 2), (rows, 1), 0, top)
    return jnp.take_along_axis(grid, (jnp.arange(top)[None, :] + offset_by) % top, axis=1)


def load_shares(number_of, total, most, slope, full):
    weights = [(1 << 20) // math.isqrt(grade ** slope) + 1 for grade in range(1, number_of + 1)]
    largest = most if full else min(most, max(-(-total // number_of), total * weights[0] // sum(weights)))
    least = 1 if total - largest >= number_of - 1 else 0
    holding, spare = [largest] + [least] * (number_of - 1), total - largest - least * (number_of - 1)
    while spare > 0:
        candidates = [i for i in range(1, number_of) if holding[i] < largest] or [i for i in range(1, number_of) if holding[i] < most]
        whole, remaining = sum([weights[i] for i in candidates]), spare
        for i in candidates:
            addition = min(most - holding[i], max(1, remaining * weights[i] // whole), spare)
            holding[i] = holding[i] + addition
            spare = spare - addition
    return np.array(holding)


def bell_draw(own_key, shape, spread, most, cuts=(), held_as=jnp.bfloat16):
    result = jax.random.normal(own_key, shape, jnp.float32) * spread
    if len(cuts) > 0:
        result = block_levels(own_key, shape, cuts, -0.22, 0.18) * result
    return jnp.clip(result, min=-most, max=most).astype(held_as)


def setup_inputs(seed: int = 0) -> dict:
    streams_of = jax.random.split(jax.random.key(seed), 10)
    tokens = bell_draw(streams_of[0], (TOKENS, D), 1.0, 6.0, ((0, 128),))
    expert_ids_keys = jax.random.split(jax.random.fold_in(streams_of[1], 1), TOKENS // TOK_DEV)
    expert_ids_turns = jax.random.permutation(jax.random.fold_in(streams_of[1], 3), TOKENS // TOK_DEV)
    expert_ids = jax.vmap(lambda own, number: assign_block(jax.random.fold_in(streams_of[1], 2), own, number, TOK_DEV, EXPERTS, 3, CAP, 2))(expert_ids_keys, expert_ids_turns).reshape((TOKENS, 3))
    gate_values = jnp.clip(0.2 + 1.3 * jax.random.uniform(streams_of[2], (TOKENS, 3), jnp.float32) ** block_levels(streams_of[2], (TOKENS, 3), ((0, 128),), -0.2, 0.2), 0.2, 1.5)
    shared_gate = bell_draw(streams_of[3], (D, FS), D ** -0.5, 0.0625, ((1, 32),))
    shared_up = bell_draw(streams_of[4], (D, FS), D ** -0.5, 0.0625, ((1, 32),))
    shared_down = bell_draw(streams_of[5], (FS, D), FS ** -0.5, 0.078125, ((0, 32),))
    routed_gate = bell_draw(streams_of[6], (N_FFN, D, FF_HALF), D ** -0.5, 0.0625, ((0, 32), (2, 4)))
    routed_up = bell_draw(streams_of[7], (N_FFN, D, FF_HALF), D ** -0.5, 0.0625, ((0, 32), (2, 4)))
    routed_down = bell_draw(streams_of[8], (N_FFN, FF_HALF, D), FF_WIN ** -0.5, 0.125, ((0, 32), (1, 4)))
    return {"tokens": tokens, "expert_ids": expert_ids, "gate_values": gate_values, "shared_gate": shared_gate, "shared_up": shared_up, "shared_down": shared_down, "routed_gate": routed_gate, "routed_up": routed_up, "routed_down": routed_down}


def reference(tokens, expert_ids, gate_values, shared_gate, shared_up, shared_down, routed_gate, routed_up, routed_down):
    gate_part = jnp.dot(tokens, shared_gate, preferred_element_type=jnp.float32)
    up_part = jnp.dot(tokens, shared_up, preferred_element_type=jnp.float32)
    shared_hidden = (jax.nn.silu(gate_part) * up_part).astype(jnp.bfloat16)
    shared_out = jnp.dot(shared_hidden, shared_down, preferred_element_type=jnp.float32)
    flat_ids = expert_ids.reshape(-1)
    limit = N_ATTN * N_FFN * CAP

    def one_expert(carry, expert):
        chosen = flat_ids == expert
        picked = jnp.nonzero(chosen, size=limit, fill_value=0)[0]
        valid = jnp.arange(limit) < jnp.sum(chosen.astype(jnp.int32))
        block_rows = tokens[picked // 3]
        total = jnp.zeros((limit, D), jnp.float32)
        for half_index in range(2):
            owner = expert + half_index * EXPERTS
            gate_rows = jnp.dot(block_rows, routed_gate[owner], preferred_element_type=jnp.float32)
            up_rows = jnp.dot(block_rows, routed_up[owner], preferred_element_type=jnp.float32)
            hidden = (jax.nn.silu(gate_rows) * up_rows).astype(jnp.bfloat16)
            half_out = jnp.dot(hidden, routed_down[owner], preferred_element_type=jnp.float32).astype(jnp.bfloat16)
            total = total + half_out.astype(jnp.float32)
        carry = carry.at[picked].add(jnp.where(valid[:, None], total, jnp.zeros_like(total)))
        return carry, None

    paired = lax.scan(one_expert, jnp.zeros((TOKENS * 3, D), jnp.float32), jnp.arange(EXPERTS))[0]
    routed_out = jnp.sum(gate_values[:, :, None] * paired.reshape(TOKENS, 3, D), axis=1)
    return (shared_out + routed_out).astype(jnp.bfloat16)
```

```python
import jax
import jax.numpy as jnp
from jax import lax
from jax.experimental import pallas as pl
from jax.experimental.pallas import tpu as pltpu
from jax.sharding import PartitionSpec as P

MESH = pl.DeviceIdType.MESH
BF16, F32 = jnp.bfloat16, jnp.float32

D = 7168
HALF = D // 2
EXTRA = 128
WIDE = HALF + EXTRA
T_OFF, T_WIDTH = (0, 1280, 2560), (1280, 1280, 1152)
K_OFF, K_WIDTH = (0, 1280, 2432), (1280, 1152, 1152)
GATE_AT = 2432
ORDER = ((0, 2, 1), (2, 1, 0), (1, 0, 2))
ROUTED, SHARED, HIDDEN = 320, 160, 512
UP = 384


def kernel(
    tok, ids, gv, sg, su, sd, rg, ru, rd, out,
    T, W, SG, SU, WD, ACC, ASG, ASU, H, SIB, RL, RD, R2, R3, MINE, XR, FIN, FR,
    w_sem, x_sem, p1_s, p1_r, p2_s, p2_r, p3_s, p3_r, rl_s, rl_r, sb_s, sb_r,
    pr_s, pr_r, op_s, op_r, di_s, di_r, q2_s, q2_r, q3_s, q3_r,
):
    cy = lax.axis_index("attn")
    f = lax.axis_index("ffn")
    cx, cz, c = f // 8, (f // 2) % 4, f % 2
    here = (cy, cx, cz)

    def chip(dim, step):
        at = list(here)
        at[dim] = (at[dim] + step) % 4
        return {"attn": at[0], "ffn": (at[1] * 4 + at[2]) * 2 + c}

    sibling = {"attn": cy, "ffn": f + 1 - 2 * c}

    def send(src, dst, s, r, where):
        return pltpu.make_async_remote_copy(
            src_ref=src, dst_ref=dst, send_sem=s, recv_sem=r, device_id=where, device_id_type=MESH
        )

    loads = [
        pltpu.make_async_copy(rg.at[0], W.at[pl.ds(0, ROUTED)], w_sem.at[0]),
        pltpu.make_async_copy(ru.at[0], W.at[pl.ds(UP, ROUTED)], w_sem.at[1]),
        pltpu.make_async_copy(sg, SG, w_sem.at[2]),
        pltpu.make_async_copy(su, SU, w_sem.at[3]),
        pltpu.make_async_copy(rd.at[0], WD.at[pl.ds(0, ROUTED)], w_sem.at[4]),
        pltpu.make_async_copy(sd, WD.at[pl.ds(ROUTED, SHARED)], w_sem.at[5]),
    ]
    for load in loads:
        load.start()

    barrier = pltpu.get_barrier_semaphore()
    for dim in range(3):
        for step in (1, 2, 3):
            pl.semaphore_signal(barrier, inc=1, device_id=chip(dim, step), device_id_type=MESH)
    pl.semaphore_signal(barrier, inc=1, device_id=sibling, device_id_type=MESH)

    lane = lax.broadcasted_iota(jnp.int32, (8, EXTRA), 1)
    gate = jnp.zeros((8, EXTRA), F32)
    diagonal = lax.broadcasted_iota(jnp.int32, (8, 8), 0) == lax.broadcasted_iota(jnp.int32, (8, 8), 1)
    expert_lane = (lane % 16).astype(F32)

    def column(v):
        return jnp.sum(jnp.where(diagonal, v, 0.0), axis=1, keepdims=True)

    for j in range(3):
        named = column(ids[j : j + 1, :].astype(F32))
        gate = gate + jnp.where(named == expert_lane, column(gv[j : j + 1, :]), 0.0)
    g_hi = gate.astype(BF16).astype(F32)
    g_mid = (gate - g_hi).astype(BF16).astype(F32)
    g_lo = gate - g_hi - g_mid
    gate = jnp.where(lane < 16, g_hi, jnp.where(lane < 32, g_mid, jnp.where(lane < 48, g_lo, 0.0)))

    def twice(v):
        v = v.astype(F32)
        return jnp.concatenate([v, v], axis=0).astype(BF16)

    for h in range(2):
        MINE[h, :, 0:GATE_AT] = twice(tok[:, h * HALF : h * HALF + GATE_AT])
        MINE[h, :, GATE_AT : GATE_AT + EXTRA] = twice(gate)
        MINE[h, :, GATE_AT + EXTRA : WIDE] = twice(tok[:, h * HALF + GATE_AT : (h + 1) * HALF])

    pl.semaphore_wait(barrier, 10)
    swap = send(MINE.at[1 - c], XR, x_sem.at[0], x_sem.at[1], sibling)
    swap.start()

    WD[ROUTED + SHARED : HIDDEN, :] = jnp.zeros((HIDDEN - ROUTED - SHARED, D), BF16)
    H[...] = jnp.zeros(H.shape, BF16)

    def clear(i, carry):
        ACC[i] = jnp.zeros(ACC.shape[1:], F32)
        return carry

    lax.fori_loop(0, 4, clear, 0)
    ASG[...] = jnp.zeros(ASG.shape, F32)
    ASU[...] = jnp.zeros(ASU.shape, F32)

    swap.wait()
    row = lax.broadcasted_iota(jnp.int32, (16, WIDE), 0)
    chunk = jnp.where(row // 8 == c, MINE[c].astype(F32), XR[...].astype(F32)).astype(BF16)
    T[cy, cx, cz, :, pl.ds(pl.multiple_of(c * WIDE, 128), WIDE)] = chunk

    def wide_cols(half, p):
        return pl.ds(pl.multiple_of(half * WIDE + T_OFF[p], 128), T_WIDTH[p])

    def t_cols(half, p):
        return pl.ds(pl.multiple_of(half * WIDE + T_OFF[p], 128), K_WIDTH[p])

    def d_cols(half, p):
        return pl.ds(pl.multiple_of(half * HALF + K_OFF[p], 128), K_WIDTH[p])

    def part_cols(p):
        return pl.ds(K_OFF[p], K_WIDTH[p])

    def place(p, a, b, cc):
        at = [None] * 3
        for dim, i in zip(ORDER[p], (a, b, cc)):
            at[dim] = slice(None) if i is None else i
        return tuple(at)

    def plane(p, cc, j=None):
        at = list(place(p, None, None, cc))
        if j is not None:
            at[min(ORDER[p][:2])] = pl.ds(2 * j, 2)
        return tuple(at)

    def own(p):
        return tuple(here[dim] for dim in ORDER[p])

    def offset(g):
        return (g * (g + 1) // 2) % 4

    def group(p, g):
        return (own(p)[2] + offset(g)) % 4

    parts = range(3)

    def first(p, k):
        at = place(p, *own(p)) + (slice(None), wide_cols(c, p))
        return send(T.at[at], T.at[at], p1_s.at[p, k - 1], p1_r.at[p, k - 1], chip(ORDER[p][0], k))

    def second(p, k):
        a, b, cc = own(p)
        at = place(p, None, b, cc) + (slice(None), wide_cols(c, p))
        return send(T.at[at], T.at[at], p2_s.at[p, k - 1], p2_r.at[p, k - 1], chip(ORDER[p][1], k))

    def third(p, d, j):
        at = plane(p, own(p)[2], j) + (slice(None), wide_cols(c, p))
        return send(
            T.at[at], T.at[at], p3_s.at[p, d, j], p3_r.at[p, d, j], chip(ORDER[p][2], (1, 3)[d])
        )

    def relay(p, d):
        at = plane(p, (own(p)[2] + (3, 1)[d]) % 4, d) + (slice(None), wide_cols(c, p))
        return send(T.at[at], T.at[at], rl_s.at[p, d], rl_r.at[p, d], chip(ORDER[p][2], (1, 3)[d]))

    def share(p, g, j):
        at = plane(p, group(p, g), j) + (slice(None), wide_cols(c, p))
        return send(T.at[at], T.at[at], sb_s.at[p, g, j], sb_r.at[p, g, j], sibling)

    steps = (1, 3, 2)
    for p in parts:
        for k in steps:
            first(p, k).start()
    for p in parts:
        for k in steps:
            first(p, k).wait_recv()
        for k in steps:
            second(p, k).start()
    for p in parts:
        for k in steps:
            second(p, k).wait_recv()
        for d in range(2):
            third(p, d, d).start()
        for d in range(2):
            third(p, d, 1 - d).start()
        for j in range(2):
            share(p, 0, j).start()
    for load in loads:
        load.wait()

    def times(rows, weights):
        return lax.dot_general(rows, weights, (((1,), (1,)), ((), ())), preferred_element_type=F32)

    def gather_step(g, carry):
        @pl.when(g == 1)
        def _():
            for p in parts:
                for d in range(2):
                    third(p, d, d).wait_recv()
                    relay(p, d).start()
                    share(p, 2 - d, d).start()
            for p in parts:
                third(p, 1, 0).wait_recv()
                share(p, 1, 0).start()

        @pl.when(g == 2)
        def _():
            for p in parts:
                third(p, 0, 1).wait_recv()
                share(p, 2, 1).start()

        @pl.when(g == 3)
        def _():
            for p in parts:
                for d in range(2):
                    relay(p, d).wait_recv()
                    share(p, 3, d).start()

        def project(turn, carry):
            half = (c + turn) % 2
            for p in parts:

                @pl.when(turn == 1)
                def _():
                    for j in range(2):
                        share(p, g, j).wait_recv()

                at = plane(p, group(p, g)) + (slice(None),)
                rows = T[at + (t_cols(half, p),)].reshape(256, K_WIDTH[p])
                depth = d_cols(half, p)
                ACC[at + (slice(None),)] += times(rows, W[:, depth]).reshape(4, 4, 16, UP + ROUTED)
            return carry

        lax.fori_loop(0, 2, project, 0)
        return carry

    lax.fori_loop(0, 4, gather_step, 0)

    for p in parts:
        for k in steps:
            first(p, k).wait_send()
            second(p, k).wait_send()
        for d in range(2):
            relay(p, d).wait_send()
            for j in range(2):
                third(p, d, j).wait_send()
        for g in range(4):
            for j in range(2):
                share(p, g, j).wait_send()

    def project_shared(half, carry):
        for p in parts:
            rows = T[cy, :, :, :, t_cols(half, p)].reshape(256, K_WIDTH[p])
            depth = d_cols(half, p)
            ASG[...] += times(rows, SG[:, depth])
            ASU[...] += times(rows, SU[:, depth])
        return carry

    lax.fori_loop(0, 2, project_shared, 0)

    expert = f % 16
    gate_lane = lax.broadcasted_iota(jnp.int32, (256, EXTRA), 1)
    chosen = jnp.logical_and(gate_lane % 16 == expert, gate_lane < 48)

    def silu(v):
        return v / (1.0 + jnp.exp(-v))

    def hide(y, carry):
        gates = T[y, :, :, :, GATE_AT : GATE_AT + EXTRA].reshape(256, EXTRA).astype(F32)
        weight = jnp.sum(jnp.where(chosen, gates, 0.0), axis=1, keepdims=True)
        v = ACC[y, :, :, :, 0:ROUTED].reshape(256, ROUTED)
        u = ACC[y, :, :, :, UP : UP + ROUTED].reshape(256, ROUTED)
        H[y, :, :, :, 0:ROUTED] = (silu(v) * u * weight).astype(BF16).reshape(4, 4, 16, ROUTED)
        return carry

    lax.fori_loop(0, 4, hide, 0)
    mine = silu(ASG[...]) * ASU[...]
    mine = jnp.concatenate(
        [jnp.zeros((256, ROUTED), F32), mine, jnp.zeros((256, HIDDEN - ROUTED - SHARED), F32)], axis=1
    )
    H[cy] = (H[cy].astype(F32) + mine.reshape(4, 4, 16, HIDDEN)).astype(BF16)

    def pair(p, g):
        at = plane(p, group(p, g)) + (slice(None),)
        return send(
            T.at[at + (t_cols(1 - c, p),)], SIB.at[at + (part_cols(p),)], pr_s.at[p, g], pr_r.at[p, g], sibling
        )

    def opposite(p, j):
        at = plane(p, group(p, 3), j) + (slice(None), t_cols(c, p))
        return send(
            T.at[at], RL.at[(j, slice(None), slice(None), slice(None), part_cols(p))],
            op_s.at[p, j], op_r.at[p, j], chip(ORDER[p][2], (1, 3)[j]),
        )

    def direct(p, d):
        at = plane(p, group(p, 1 + d)) + (slice(None), t_cols(c, p))
        return send(
            T.at[at], RD.at[(d, slice(None), slice(None), slice(None), part_cols(p))],
            di_s.at[p, d], di_r.at[p, d], chip(ORDER[p][2], (1, 3)[d]),
        )

    def back_second(p, k):
        a, b, cc = own(p)
        at = place(p, None, (b + k) % 4, cc) + (slice(None), t_cols(c, p))
        return send(
            T.at[at], R2.at[(k - 1, slice(None), slice(None), part_cols(p))],
            q2_s.at[p, k - 1], q2_r.at[p, k - 1], chip(ORDER[p][1], k),
        )

    def back_first(p, k):
        a, b, cc = own(p)
        at = place(p, (a + k) % 4, b, cc) + (slice(None), t_cols(c, p))
        return send(
            T.at[at], R3.at[(k - 1, slice(None), part_cols(p))],
            q3_s.at[p, k - 1], q3_r.at[p, k - 1], chip(ORDER[p][0], k),
        )

    def down(p, g, half):
        at = plane(p, group(p, g)) + (slice(None), slice(None))
        return jnp.dot(
            H[at].reshape(256, HIDDEN), WD[:, d_cols(half, p)], preferred_element_type=F32
        ).reshape(4, 4, 16, K_WIDTH[p])

    def for_sibling(g):
        for p in parts:
            T[plane(p, group(p, g)) + (slice(None), t_cols(1 - c, p))] = down(p, g, 1 - c).astype(BF16)
            pair(p, g).start()

    def scatter_step(r, carry):
        g = 4 - r

        @pl.when(r < 4)
        def _():
            for_sibling(g - 1)

        @pl.when(r > 0)
        def _():
            for p in parts:
                pair(p, g).wait_recv()

                for d in range(2):

                    @pl.when(g == 1 + d)
                    def _():
                        opposite(p, d).wait_recv()
                        at = plane(p, group(p, g), d) + (slice(None), part_cols(p))
                        SIB[at] = (SIB[at].astype(F32) + RL[d, :, :, :, part_cols(p)].astype(F32)).astype(BF16)

                at = plane(p, group(p, g)) + (slice(None),)
                T[at + (t_cols(c, p),)] = (
                    down(p, g, c) + SIB[at + (part_cols(p),)].astype(F32)
                ).astype(BF16)

                @pl.when(g == 3)
                def _():
                    for j in range(2):
                        opposite(p, j).start()

                for d in range(2):

                    @pl.when(g == 1 + d)
                    def _():
                        direct(p, d).start()

        return carry

    lax.fori_loop(0, 5, scatter_step, 0)

    for p in parts:
        for d in range(2):
            direct(p, d).wait_recv()
        at = plane(p, own(p)[2]) + (slice(None), t_cols(c, p))
        total = T[at].astype(F32)
        for d in range(2):
            total = total + RD[d, :, :, :, part_cols(p)].astype(F32)
        T[at] = total.astype(BF16)
        for k in steps:
            back_second(p, k).start()
    for p in parts:
        for k in steps:
            back_second(p, k).wait_recv()
        a, b, cc = own(p)
        at = place(p, None, b, cc) + (slice(None), t_cols(c, p))
        total = T[at].astype(F32)
        for k in steps:
            total = total + R2[k - 1, :, :, part_cols(p)].astype(F32)
        T[at] = total.astype(BF16)
        for k in steps:
            back_first(p, k).start()
    for p in parts:
        for k in steps:
            back_first(p, k).wait_recv()
        at = place(p, *own(p)) + (slice(None), t_cols(c, p))
        total = T[at].astype(F32)
        for k in steps:
            total = total + R3[k - 1, :, part_cols(p)].astype(F32)
        FIN[:, part_cols(p)] = total.astype(BF16)
    finish = send(FIN, FR, x_sem.at[2], x_sem.at[3], sibling)
    finish.start()

    def my_rows(v):
        v = v.astype(F32)
        return jnp.where(c == 0, v[0:8], v[8:16]).astype(BF16)

    out[:, pl.ds(pl.multiple_of(c * HALF, 128), HALF)] = my_rows(FIN[...])
    finish.wait_recv()
    out[:, pl.ds(pl.multiple_of((1 - c) * HALF, 128), HALF)] = my_rows(FR[...])

    finish.wait_send()
    for p in parts:
        for g in range(4):
            pair(p, g).wait_send()
        for d in range(2):
            opposite(p, d).wait_send()
            direct(p, d).wait_send()
        for k in steps:
            back_second(p, k).wait_send()
            back_first(p, k).wait_send()


def shards(tok, ids, gv, sg, su, sd, rg, ru, rd):
    def turned(v):
        return jnp.swapaxes(v, -1, -2)

    arrays = (tok, turned(ids), turned(gv), turned(sg), turned(su), sd, turned(rg), turned(ru), rd)
    dma = pltpu.SemaphoreType.DMA
    vmem = pl.BlockSpec(memory_space=pltpu.VMEM)
    hbm = pl.BlockSpec(memory_space=pl.ANY)
    return pl.pallas_call(
        kernel,
        out_shape=jax.ShapeDtypeStruct((8, D), BF16),
        in_specs=[vmem] * 3 + [hbm] * 6,
        out_specs=vmem,
        scratch_shapes=[
            pltpu.VMEM((4, 4, 4, 16, 2 * WIDE), BF16),
            pltpu.VMEM((UP + ROUTED, D), BF16),
            pltpu.VMEM((SHARED, D), BF16),
            pltpu.VMEM((SHARED, D), BF16),
            pltpu.VMEM((HIDDEN, D), BF16),
            pltpu.VMEM((4, 4, 4, 16, UP + ROUTED), F32),
            pltpu.VMEM((256, SHARED), F32),
            pltpu.VMEM((256, SHARED), F32),
            pltpu.VMEM((4, 4, 4, 16, HIDDEN), BF16),
            pltpu.VMEM((4, 4, 4, 16, HALF), BF16),
            pltpu.VMEM((2, 2, 4, 16, HALF), BF16),
            pltpu.VMEM((2, 4, 4, 16, HALF), BF16),
            pltpu.VMEM((3, 4, 16, HALF), BF16),
            pltpu.VMEM((3, 16, HALF), BF16),
            pltpu.VMEM((2, 16, WIDE), BF16),
            pltpu.VMEM((16, WIDE), BF16),
            pltpu.VMEM((16, HALF), BF16),
            pltpu.VMEM((16, HALF), BF16),
            dma((6,)), dma((4,)),
            dma((3, 3)), dma((3, 3)), dma((3, 3)), dma((3, 3)),
            dma((3, 2, 2)), dma((3, 2, 2)), dma((3, 2)), dma((3, 2)), dma((3, 4, 2)), dma((3, 4, 2)),
            dma((3, 4)), dma((3, 4)), dma((3, 2)), dma((3, 2)), dma((3, 2)), dma((3, 2)),
            dma((3, 3)), dma((3, 3)), dma((3, 3)), dma((3, 3)),
        ],
        compiler_params=pltpu.CompilerParams(
            collective_id=0, has_side_effects=True, vmem_limit_bytes=62 << 20
        ),
        name="moe_ffn",
    )(*arrays)


def solution(mesh):
    placed = (
        P(("attn", "ffn"), None),
        P(("attn", "ffn"), None),
        P(("attn", "ffn"), None),
        P(None, "ffn"),
        P(None, "ffn"),
        P("ffn", None),
        P("ffn", None, "attn"),
        P("ffn", None, "attn"),
        P("ffn", "attn", None),
    )
    return jax.shard_map(
        shards, mesh=mesh, in_specs=placed, out_specs=P(("attn", "ffn"), None), check_vma=False
    )
```

```python
import jax
import jax.numpy as jnp
from jax import lax
from jax.experimental import pallas as pl
from jax.experimental.pallas import tpu as pltpu
from jax.sharding import PartitionSpec as P

MESH = pl.DeviceIdType.MESH
BF16, F32 = jnp.bfloat16, jnp.float32

D = 7168
HALF = D // 2
EXTRA = 128
WIDE = HALF + EXTRA
T_OFF, T_WIDTH = (0, 1280, 2560), (1280, 1280, 1152)
K_OFF, K_WIDTH = (0, 1280, 2432), (1280, 1152, 1152)
GATE_AT = 2432
ORDER = ((0, 2, 1), (2, 1, 0), (1, 0, 2))
ROUTED, SHARED, HIDDEN = 320, 160, 512
UP = 384


def kernel(
    tok_hbm, ids_hbm, gv_hbm, sg, su, sd, rg, ru, rd, out,
    T, W, SG, SU, WD, ACC, ASG, ASU, H, SUM, RL, RD, R2, R3, RB, tok, ids, gv, MINE, XR, FIN, FR,
    w_sem, i_sem, x_sem, p1_s, p1_r, p2_s, p2_r, re_s, re_r, p0_s, p0_r, p3_s, p3_r, rl_s, rl_r, sb_s, sb_r,
    pr_s, pr_r, op_s, op_r, di_s, di_r, q2_s, q2_r, qo_s, qo_r, q3_s, q3_r, ready,
):
    cy = lax.axis_index("attn")
    f = lax.axis_index("ffn")
    cx, cz, c = f // 8, (f // 2) % 4, f % 2
    here = (cy, cx, cz)

    def chip(dim, step):
        at = list(here)
        at[dim] = (at[dim] + step) % 4
        return {"attn": at[0], "ffn": (at[1] * 4 + at[2]) * 2 + c}

    sibling = {"attn": cy, "ffn": f + 1 - 2 * c}

    def send(src, dst, s, r, where):
        return pltpu.make_async_remote_copy(
            src_ref=src, dst_ref=dst, send_sem=s, recv_sem=r, device_id=where, device_id_type=MESH
        )

    inputs = [
        pltpu.make_async_copy(tok_hbm, tok, i_sem.at[0]),
        pltpu.make_async_copy(ids_hbm, ids, i_sem.at[1]),
        pltpu.make_async_copy(gv_hbm, gv, i_sem.at[2]),
    ]
    for copy in inputs:
        copy.start()

    barrier = pltpu.get_barrier_semaphore()
    for dim in range(3):
        for step in (1, 2, 3):
            pl.semaphore_signal(barrier, inc=1, device_id=chip(dim, step), device_id_type=MESH)
    pl.semaphore_signal(barrier, inc=1, device_id=sibling, device_id_type=MESH)

    loads = [
        pltpu.make_async_copy(rg.at[0], W.at[pl.ds(0, ROUTED // 16)], w_sem.at[0]),
        pltpu.make_async_copy(ru.at[0], W.at[pl.ds(UP // 16, ROUTED // 16)], w_sem.at[1]),
        pltpu.make_async_copy(sg, SG, w_sem.at[2]),
        pltpu.make_async_copy(su, SU, w_sem.at[3]),
        pltpu.make_async_copy(rd.at[0], WD.at[pl.ds(0, ROUTED)], w_sem.at[4]),
        pltpu.make_async_copy(sd, WD.at[pl.ds(ROUTED, SHARED)], w_sem.at[5]),
    ]
    for load in loads:
        load.start()
    for copy in inputs:
        copy.wait()

    lane = lax.broadcasted_iota(jnp.int32, (8, EXTRA), 1)
    gate = jnp.zeros((8, EXTRA), F32)
    diagonal = lax.broadcasted_iota(jnp.int32, (8, 8), 0) == lax.broadcasted_iota(jnp.int32, (8, 8), 1)
    expert_lane = (lane % 16).astype(F32)

    def column(v):
        return jnp.sum(jnp.where(diagonal, v, 0.0), axis=1, keepdims=True)

    for j in range(3):
        named = column(ids[j : j + 1, :].astype(F32))
        gate = gate + jnp.where(named == expert_lane, column(gv[j : j + 1, :]), 0.0)
    g_hi = gate.astype(BF16).astype(F32)
    g_mid = (gate - g_hi).astype(BF16).astype(F32)
    g_lo = gate - g_hi - g_mid
    gate = jnp.where(lane < 16, g_hi, jnp.where(lane < 32, g_mid, jnp.where(lane < 48, g_lo, 0.0)))

    def twice(v):
        v = v.astype(F32)
        return jnp.concatenate([v, v], axis=0).astype(BF16)

    for h in range(2):
        MINE[h, :, 0:GATE_AT] = twice(tok[:, h * HALF : h * HALF + GATE_AT])
        MINE[h, :, GATE_AT : GATE_AT + EXTRA] = twice(gate)
        MINE[h, :, GATE_AT + EXTRA : WIDE] = twice(tok[:, h * HALF + GATE_AT : (h + 1) * HALF])

    pl.semaphore_wait(barrier, 10)
    swap = send(MINE.at[1 - c], XR, x_sem.at[0], x_sem.at[1], sibling)
    swap.start()

    WD[ROUTED + SHARED : HIDDEN, :] = jnp.zeros((HIDDEN - ROUTED - SHARED, D), BF16)
    H[...] = jnp.zeros(H.shape, BF16)

    def clear(i, carry):
        ACC[i] = jnp.zeros(ACC.shape[1:], F32)
        return carry

    lax.fori_loop(0, 4, clear, 0)
    ASG[...] = jnp.zeros(ASG.shape, F32)
    ASU[...] = jnp.zeros(ASU.shape, F32)

    swap.wait()
    row = lax.broadcasted_iota(jnp.int32, (16, WIDE), 0)
    chunk = jnp.where(row // 8 == c, MINE[c].astype(F32), XR[...].astype(F32)).astype(BF16)
    T[cy, cx, cz, :, pl.ds(pl.multiple_of(c * WIDE, 128), WIDE)] = chunk

    def wide_cols(half, p):
        return pl.ds(pl.multiple_of(half * WIDE + T_OFF[p], 128), T_WIDTH[p])

    def t_cols(half, p):
        return pl.ds(pl.multiple_of(half * WIDE + T_OFF[p], 128), K_WIDTH[p])

    def d_cols(half, p):
        return pl.ds(pl.multiple_of(half * HALF + K_OFF[p], 128), K_WIDTH[p])

    def part_cols(p):
        return pl.ds(K_OFF[p], K_WIDTH[p])

    def place(p, a, b, cc):
        at = [None] * 3
        for dim, i in zip(ORDER[p], (a, b, cc)):
            at[dim] = slice(None) if i is None else i
        return tuple(at)

    def plane(p, cc, j=None):
        at = list(place(p, None, None, cc))
        if j is not None:
            at[min(ORDER[p][:2])] = pl.ds(2 * j, 2)
        return tuple(at)

    def own(p):
        return tuple(here[dim] for dim in ORDER[p])

    def offset(i):
        return (i * (i + 1) // 2) % 4

    def group(p, g):
        return (own(p)[2] + offset(g)) % 4

    def line(p, g, s):
        return place(p, None, (own(p)[1] + offset(s)) % 4, group(p, g)) + (slice(None),)

    parts = range(3)
    steps = (1, 3, 2)
    ROUTE = (0, 1, 1, 0)
    BACK = (2, 1)

    def first(p, k):
        at = place(p, *own(p)) + (slice(None), wide_cols(c, p))
        return send(T.at[at], T.at[at], p1_s.at[p, k - 1], p1_r.at[p, k - 1], chip(ORDER[p][0], k))

    def chunk_at(p, g, s, i):
        a, b, _ = own(p)
        return place(p, (a + offset(i)) % 4, (b + offset(s)) % 4, group(p, g)) + (slice(None),)

    def second(p, d, i):
        at = chunk_at(p, 0, 0, i) + (wide_cols(c, p),)
        return send(
            T.at[at], T.at[at], p2_s.at[p, d, i], p2_r.at[p, d, i], chip(ORDER[p][1], (1, 3)[d])
        )

    def second_relay(p, i):
        d = ROUTE[i]
        at = chunk_at(p, 0, BACK[d], i) + (wide_cols(c, p),)
        return send(T.at[at], T.at[at], re_s.at[p, i], re_r.at[p, i], chip(ORDER[p][1], (1, 3)[d]))

    def third_chunk(p, d, i):
        at = chunk_at(p, 0, 0, i) + (wide_cols(c, p),)
        return send(
            T.at[at], T.at[at], p0_s.at[p, d, i], p0_r.at[p, d, i], chip(ORDER[p][2], (1, 3)[d])
        )

    def third(p, d, s):
        at = line(p, 0, s) + (wide_cols(c, p),)
        return send(
            T.at[at], T.at[at], p3_s.at[p, d, s - 1], p3_r.at[p, d, s - 1], chip(ORDER[p][2], (1, 3)[d])
        )

    def relay(p, s):
        d = ROUTE[s]
        at = line(p, BACK[d], s) + (wide_cols(c, p),)
        return send(T.at[at], T.at[at], rl_s.at[p, s], rl_r.at[p, s], chip(ORDER[p][2], (1, 3)[d]))

    def share(p, g, s):
        at = line(p, g, s) + (wide_cols(c, p),)
        return send(T.at[at], T.at[at], sb_s.at[p, g, s], sb_r.at[p, g, s], sibling)

    for p in parts:
        for k in steps:
            first(p, k).start()
    for p in parts:
        for d in range(2):
            second(p, d, 0).start()
    for p in parts:
        for d in range(2):
            third_chunk(p, d, 0).start()
    for k, i in ((3, 1), (1, 2), (2, 3)):
        for p in parts:
            first(p, k).wait_recv()
            for d in range(2):
                second(p, d, i).start()
    for p in parts:
        for i in (1, 2, 3):
            for d in range(2):
                third_chunk(p, d, i).start()
        share(p, 0, 0).start()
    for i in range(4):
        for p in parts:
            for d in range(2):
                second(p, d, i).wait_recv()
                if ROUTE[i] == d:
                    second_relay(p, i).start()
    for s in (1, 2):
        for p in parts:
            for d in range(2):
                third(p, d, s).start()
            share(p, 0, s).start()
    for p in parts:
        for i in range(4):
            second_relay(p, i).wait_recv()
        for d in range(2):
            third(p, d, 3).start()
        share(p, 0, 3).start()
    for load in loads:
        load.wait()

    def times(rows, weights):
        weights = weights.reshape(-1, weights.shape[-1])
        return lax.dot_general(rows, weights, (((1,), (1,)), ((), ())), preferred_element_type=F32)

    def pass_on(s):
        for p in parts:
            for d in range(2):
                if s == 0:
                    for i in range(4):
                        third_chunk(p, d, i).wait_recv()
                else:
                    third(p, d, s).wait_recv()
                if ROUTE[s] == d:
                    relay(p, s).start()
                share(p, BACK[d], s).start()

    def take_in(s):
        for p in parts:
            relay(p, s).wait_recv()
            share(p, 3, s).start()

    def gather_step(q, carry):
        m, turn = q // 2, q % 2
        half = (c + turn) % 2
        mixed = (m + 1) // 2 % 2
        lines = [
            (m * (1 - mixed) + mixed * (1 + i // 2), i * (1 - mixed) + mixed * (2 * (m - 1) + i % 2))
            for i in range(4)
        ]

        for s in range(4):

            @pl.when(q == 1 + s)
            def _():
                pass_on(s)

        @pl.when(q == 5)
        def _():
            take_in(0)

        @pl.when(q == 6)
        def _():
            for s in (1, 2, 3):
                take_in(s)

        for p in parts:

            @pl.when(turn == 1)
            def _():
                for g, s in lines:
                    share(p, g, s).wait_recv()

            cols, depth = t_cols(half, p), d_cols(half, p)
            places = [line(p, g, s) for g, s in lines]
            rows = jnp.concatenate([T[at + (cols,)].reshape(64, K_WIDTH[p]) for at in places], axis=0)
            product = times(rows, W[:, :, depth])
            for i, at in enumerate(places):
                ACC[at + (slice(None),)] += product[64 * i : 64 * i + 64].reshape(4, 16, UP + ROUTED)

            def shared(*places):
                rows = [T[(cy,) + at + (slice(None), cols)] for at in places]
                shape = rows[0].shape[:-1]
                count = shape[0] * shape[1] * (shape[2] if len(shape) == 3 else 1)
                rows = jnp.concatenate([v.reshape(count, K_WIDTH[p]) for v in rows], axis=0)
                gate, up = times(rows, SG[:, depth]), times(rows, SU[:, depth])
                for i, at in enumerate(places):
                    at = at + (slice(None), slice(None))
                    ASG[at] += gate[count * i : count * i + count].reshape(shape + (SHARED,))
                    ASU[at] += up[count * i : count * i + count].reshape(shape + (SHARED,))

            if ORDER[p][2] == 0:

                @pl.when(m == 0)
                def _():
                    shared((slice(None), slice(None)))

            else:

                @pl.when(m % 3 == 0)
                def _():
                    shared(plane(p, group(p, m))[1:])

                @pl.when(m == 2)
                def _():
                    shared(plane(p, group(p, 1))[1:], plane(p, group(p, 2))[1:])

        return carry

    lax.fori_loop(0, 8, gather_step, 0)
    pl.semaphore_signal(ready, inc=1, device_id=sibling, device_id_type=MESH)

    for p in parts:
        for k in steps:
            first(p, k).wait_send()
        for s in range(4):
            relay(p, s).wait_send()
            second_relay(p, s).wait_send()
            for d in range(2):
                second(p, d, s).wait_send()
                third_chunk(p, d, s).wait_send()
                if s > 0:
                    third(p, d, s).wait_send()
            for g in range(4):
                share(p, g, s).wait_send()

    expert = f % 16
    gate_lane = lax.broadcasted_iota(jnp.int32, (256, EXTRA), 1)
    chosen = jnp.logical_and(gate_lane % 16 == expert, gate_lane < 48)

    def silu(v):
        return v / (1.0 + jnp.exp(-v))

    def hide(y, carry):
        gates = T[y, :, :, :, GATE_AT : GATE_AT + EXTRA].reshape(256, EXTRA).astype(F32)
        weight = jnp.sum(jnp.where(chosen, gates, 0.0), axis=1, keepdims=True)
        v = ACC[y, :, :, :, 0:ROUTED].reshape(256, ROUTED)
        u = ACC[y, :, :, :, UP : UP + ROUTED].reshape(256, ROUTED)
        H[y, :, :, :, 0:ROUTED] = (silu(v) * u * weight).astype(BF16).reshape(4, 4, 16, ROUTED)
        return carry

    lax.fori_loop(0, 4, hide, 0)
    mine = (silu(ASG[...]) * ASU[...]).reshape(256, SHARED)
    mine = jnp.concatenate(
        [jnp.zeros((256, ROUTED), F32), mine, jnp.zeros((256, HIDDEN - ROUTED - SHARED), F32)], axis=1
    )
    H[cy] = (H[cy].astype(F32) + mine.reshape(4, 4, 16, HIDDEN)).astype(BF16)

    def landed(p, g, s):
        i = g * 4 + s
        return (
            pl.ds(i % 8 * 4, 4),
            slice(None),
            pl.ds(pl.multiple_of(i // 8 * HALF + K_OFF[p], 128), K_WIDTH[p]),
        )

    def pair(p, g, s):
        at = line(p, g, s) + (t_cols(1 - c, p),)
        return send(T.at[at], W.at[landed(p, g, s)], pr_s.at[p, g, s], pr_r.at[p, g, s], sibling)

    def opposite(p, s):
        at = line(p, 3, s) + (t_cols(c, p),)
        return send(
            T.at[at], RL.at[s, :, :, part_cols(p)], op_s.at[p, s], op_r.at[p, s],
            chip(ORDER[p][2], (1, 3)[ROUTE[s]]),
        )

    def direct(p, d, s):
        at = line(p, 1 + d, s) + (t_cols(c, p),)
        return send(
            T.at[at], RD.at[d, s, :, :, part_cols(p)], di_s.at[p, d, s], di_r.at[p, d, s],
            chip(ORDER[p][2], (1, 3)[d]),
        )

    def back_second(p, s):
        at = line(p, 0, s) + (t_cols(c, p),)
        return send(
            T.at[at], R2.at[s - 1, :, :, part_cols(p)], q2_s.at[p, s - 1], q2_r.at[p, s - 1],
            chip(ORDER[p][1], offset(s)),
        )

    def back_opposite(p, i):
        at = chunk_at(p, 0, 3, i) + (t_cols(c, p),)
        return send(
            T.at[at], RB.at[i, :, part_cols(p)], qo_s.at[p, i], qo_r.at[p, i],
            chip(ORDER[p][1], (1, 3)[ROUTE[i]]),
        )

    def back_first(p, k):
        a, b, cc = own(p)
        at = place(p, (a + k) % 4, b, cc) + (slice(None), t_cols(c, p))
        return send(
            T.at[at], R3.at[k - 1, :, part_cols(p)], q3_s.at[p, k - 1], q3_r.at[p, k - 1],
            chip(ORDER[p][0], k),
        )

    def down(p, g, half):
        at = plane(p, group(p, g)) + (slice(None), slice(None))
        return jnp.dot(
            H[at].reshape(256, HIDDEN), WD[:, d_cols(half, p)], preferred_element_type=F32
        ).reshape(4, 4, 16, K_WIDTH[p])

    def sum_at(p, *at):
        a, b, _ = own(p)
        i = slice(None) if len(at) == 1 else (a + offset(at[1])) % 4
        at = ((b + offset(at[0])) % 4, i)
        return (at if ORDER[p][1] < ORDER[p][0] else at[::-1]) + (slice(None), part_cols(p))

    far_first = (3, 1, 2, 0)

    def for_sibling(g):
        for p in parts:
            T[plane(p, group(p, g)) + (slice(None), t_cols(1 - c, p))] = down(p, g, 1 - c).astype(BF16)
            for s in far_first:
                pair(p, g, s).start()

    def for_self(g, slot):
        for p in parts:
            SUM[slot, :, :, :, part_cols(p)] = down(p, g, c)

    def add_up(g, slot, s):
        for p in parts:
            pair(p, g, s).wait_recv()
            if g == 0 and s in (1, 2):
                for i in range(4):
                    if ROUTE[i] == s - 1:
                        back_opposite(p, i).wait_recv()
                        SUM[(slot,) + sum_at(p, s, i)] += RB[i, :, part_cols(p)].astype(F32)
            total = SUM[(slot,) + sum_at(p, s)] + W[landed(p, g, s)].astype(F32)
            if g in (1, 2) and ROUTE[s] == g - 1:
                opposite(p, s).wait_recv()
                total = total + RL[s, :, :, part_cols(p)].astype(F32)
            if g == 0:
                for d in range(2):
                    direct(p, d, s).wait_recv()
                    total = total + RD[d, s, :, :, part_cols(p)].astype(F32)
                if s == 0:
                    SUM[(slot,) + sum_at(p, s)] = total
                    continue
            T[line(p, g, s) + (t_cols(c, p),)] = total.astype(BF16)
            if g == 3:
                opposite(p, s).start()
            elif g > 0:
                direct(p, g - 1, s).start()
            elif s < 3:
                back_second(p, s).start()
            else:
                for i in range(4):
                    back_opposite(p, i).start()

    pl.semaphore_wait(ready, 1)

    for_sibling(3)
    for_self(3, 0)
    for s in far_first:
        add_up(3, 0, s)

    def middle(i, carry):
        for_sibling(2 - i)
        return carry

    def middle_own(i, carry):
        for_self(2 - i, i)
        return carry

    lax.fori_loop(0, 2, middle, 0)
    lax.fori_loop(0, 2, middle_own, 0)
    for s in far_first:
        for i in (0, 1) if ROUTE[s] == 0 else (1, 0):
            add_up(2 - i, i, s)
    for_sibling(0)
    for_self(0, 0)
    for s in far_first:
        add_up(0, 0, s)

    for p in parts:
        for s in (1, 2):
            back_second(p, s).wait_recv()
        total = SUM[(0,) + sum_at(p, 0)]
        for s in (1, 2):
            total = total + R2[s - 1, :, :, part_cols(p)].astype(F32)
        SUM[(0,) + sum_at(p, 0)] = total
        T[line(p, 0, 0) + (t_cols(c, p),)] = total.astype(BF16)
        for k in steps:
            back_first(p, k).start()
    for p in parts:
        for k in steps:
            back_first(p, k).wait_recv()
        total = SUM[(0,) + sum_at(p, 0, 0)]
        for k in steps:
            total = total + R3[k - 1, :, part_cols(p)].astype(F32)
        FIN[:, part_cols(p)] = total.astype(BF16)
    finish = send(FIN, FR, x_sem.at[2], x_sem.at[3], sibling)
    finish.start()

    def my_rows(v):
        v = v.astype(F32)
        return jnp.where(c == 0, v[0:8], v[8:16]).astype(BF16)

    out[:, pl.ds(pl.multiple_of(c * HALF, 128), HALF)] = my_rows(FIN[...])
    finish.wait_recv()
    out[:, pl.ds(pl.multiple_of((1 - c) * HALF, 128), HALF)] = my_rows(FR[...])

    finish.wait_send()
    for p in parts:
        for s in range(4):
            for g in range(4):
                pair(p, g, s).wait_send()
            opposite(p, s).wait_send()
            for d in range(2):
                direct(p, d, s).wait_send()
            back_opposite(p, s).wait_send()
        for s in (1, 2):
            back_second(p, s).wait_send()
        for k in steps:
            back_first(p, k).wait_send()


def shards(tok, ids, gv, sg, su, sd, rg, ru, rd):
    def turned(v):
        return jnp.swapaxes(v, -1, -2)

    def blocks(v):
        return turned(v).reshape(1, ROUTED // 16, 16, D)

    arrays = (tok, turned(ids), turned(gv), turned(sg), turned(su), sd, blocks(rg), blocks(ru), rd)
    dma = pltpu.SemaphoreType.DMA
    vmem = pl.BlockSpec(memory_space=pltpu.VMEM)
    hbm = pl.BlockSpec(memory_space=pl.ANY)
    return pl.pallas_call(
        kernel,
        out_shape=jax.ShapeDtypeStruct((8, D), BF16),
        in_specs=[hbm] * 9,
        out_specs=vmem,
        scratch_shapes=[
            pltpu.VMEM((4, 4, 4, 16, 2 * WIDE), BF16),
            pltpu.VMEM(((UP + ROUTED) // 16, 16, D), BF16),
            pltpu.VMEM((SHARED, D), BF16),
            pltpu.VMEM((SHARED, D), BF16),
            pltpu.VMEM((HIDDEN, D), BF16),
            pltpu.VMEM((4, 4, 4, 16, UP + ROUTED), F32),
            pltpu.VMEM((4, 4, 16, SHARED), F32),
            pltpu.VMEM((4, 4, 16, SHARED), F32),
            pltpu.VMEM((4, 4, 4, 16, HIDDEN), BF16),
            pltpu.VMEM((2, 4, 4, 16, HALF), F32),
            pltpu.VMEM((4, 4, 16, HALF), BF16),
            pltpu.VMEM((2, 4, 4, 16, HALF), BF16),
            pltpu.VMEM((2, 4, 16, HALF), BF16),
            pltpu.VMEM((3, 16, HALF), BF16),
            pltpu.VMEM((4, 16, HALF), BF16),
            pltpu.VMEM((8, D), BF16),
            pltpu.VMEM((3, 8), jnp.int32),
            pltpu.VMEM((3, 8), F32),
            pltpu.VMEM((2, 16, WIDE), BF16),
            pltpu.VMEM((16, WIDE), BF16),
            pltpu.VMEM((16, HALF), BF16),
            pltpu.VMEM((16, HALF), BF16),
            dma((6,)), dma((3,)), dma((4,)),
            dma((3, 3)), dma((3, 3)), dma((3, 2, 4)), dma((3, 2, 4)), dma((3, 4)), dma((3, 4)),
            dma((3, 2, 4)), dma((3, 2, 4)), dma((3, 2, 3)), dma((3, 2, 3)), dma((3, 4)), dma((3, 4)),
            dma((3, 4, 4)), dma((3, 4, 4)),
            dma((3, 4, 4)), dma((3, 4, 4)), dma((3, 4)), dma((3, 4)), dma((3, 2, 4)), dma((3, 2, 4)),
            dma((3, 2)), dma((3, 2)), dma((3, 4)), dma((3, 4)), dma((3, 3)), dma((3, 3)),
            pltpu.SemaphoreType.REGULAR,
        ],
        compiler_params=pltpu.CompilerParams(
            collective_id=0, has_side_effects=True, vmem_limit_bytes=62 << 20
        ),
        name="moe_ffn",
    )(*arrays)


def solution(mesh):
    placed = (
        P(("attn", "ffn"), None),
        P(("attn", "ffn"), None),
        P(("attn", "ffn"), None),
        P(None, "ffn"),
        P(None, "ffn"),
        P("ffn", None),
        P("ffn", None, "attn"),
        P("ffn", None, "attn"),
        P("ffn", "attn", None),
    )
    return jax.shard_map(
        shards, mesh=mesh, in_specs=placed, out_specs=P(("attn", "ffn"), None), check_vma=False
    )
```

```python
import jax
import jax.numpy as jnp
from jax import lax
from jax.experimental import pallas as pl
from jax.experimental.pallas import tpu as pltpu
from jax.sharding import PartitionSpec as P

MESH = pl.DeviceIdType.MESH
BF16, F32 = jnp.bfloat16, jnp.float32

D = 7168
HALF = D // 2
EXTRA = 128
WIDE = HALF + EXTRA
PART_AT, T_WIDTH, K_WIDTH = (0, 1280, 2560), (1280, 1280, 1152), (1280, 1280, 1024)
ORDER = ((0, 2, 1), (2, 1, 0), (1, 0, 2))
ROUTED, SHARED, HIDDEN = 320, 160, 512
UP = 384


def kernel(
    tok_hbm, ids_hbm, gv_hbm, sg, su, sd, rg, ru, rd, out,
    T, W, SG, SU, WD, ACC, ASG, ASU, H, SUM, RL, RD, R2, R3, RB, tok, ids, gv, MINE, XR, FIN, FR,
    w_sem, i_sem, x_sem, sent, p1_r, p2_r, re_r, p0_r, p3_r, rl_r, sb_r,
    pr_r, pf_r, op_r, di_r, q2_r, qo_r, q3_r, ready,
):
    cy = lax.axis_index("attn")
    f = lax.axis_index("ffn")
    cx, cz, c = f // 8, (f // 2) % 4, f % 2
    here = (cy, cx, cz)

    def chip(dim, step):
        at = list(here)
        at[dim] = (at[dim] + step) % 4
        return {"attn": at[0], "ffn": (at[1] * 4 + at[2]) * 2 + c}

    sibling = {"attn": cy, "ffn": f + 1 - 2 * c}

    def send(src, dst, s, r, where):
        return pltpu.make_async_remote_copy(
            src_ref=src, dst_ref=dst, send_sem=s, recv_sem=r, device_id=where, device_id_type=MESH
        )

    inputs = [
        pltpu.make_async_copy(tok_hbm, tok, i_sem.at[0]),
        pltpu.make_async_copy(ids_hbm, ids, i_sem.at[1]),
        pltpu.make_async_copy(gv_hbm, gv, i_sem.at[2]),
    ]
    for copy in inputs:
        copy.start()

    barrier = pltpu.get_barrier_semaphore()
    for dim in range(3):
        for step in (1, 2, 3):
            pl.semaphore_signal(barrier, inc=1, device_id=chip(dim, step), device_id_type=MESH)
    pl.semaphore_signal(barrier, inc=1, device_id=sibling, device_id_type=MESH)

    loads = [
        pltpu.make_async_copy(rg.at[0], W.at[pl.ds(0, ROUTED // 16)], w_sem.at[0]),
        pltpu.make_async_copy(ru.at[0], W.at[pl.ds(UP // 16, ROUTED // 16)], w_sem.at[1]),
        pltpu.make_async_copy(sg, SG, w_sem.at[2]),
        pltpu.make_async_copy(su, SU, w_sem.at[3]),
        pltpu.make_async_copy(rd.at[0], WD.at[pl.ds(0, ROUTED)], w_sem.at[4]),
        pltpu.make_async_copy(sd, WD.at[pl.ds(ROUTED, SHARED)], w_sem.at[5]),
    ]
    for load in loads:
        load.start()
    for copy in inputs:
        copy.wait()

    lane = lax.broadcasted_iota(jnp.int32, (8, EXTRA), 1)
    gate = jnp.zeros((8, EXTRA), F32)
    diagonal = lax.broadcasted_iota(jnp.int32, (8, 8), 0) == lax.broadcasted_iota(jnp.int32, (8, 8), 1)
    expert_lane = (lane % 16).astype(F32)

    def column(v):
        return jnp.sum(jnp.where(diagonal, v, 0.0), axis=1, keepdims=True)

    for j in range(3):
        named = column(ids[j : j + 1, :].astype(F32))
        gate = gate + jnp.where(named == expert_lane, column(gv[j : j + 1, :]), 0.0)
    g_hi = gate.astype(BF16).astype(F32)
    g_mid = (gate - g_hi).astype(BF16).astype(F32)
    g_lo = gate - g_hi - g_mid
    gate = jnp.where(lane < 16, g_hi, jnp.where(lane < 32, g_mid, jnp.where(lane < 48, g_lo, 0.0)))

    def twice(v):
        v = v.astype(F32)
        return jnp.concatenate([v, v], axis=0).astype(BF16)

    for h in range(2):
        MINE[h, :, 0:HALF] = twice(tok[:, h * HALF : (h + 1) * HALF])
        MINE[h, :, HALF:WIDE] = twice(gate)

    pl.semaphore_wait(barrier, 10)
    swap = send(MINE.at[1 - c], XR, x_sem.at[0], x_sem.at[1], sibling)
    swap.start()

    WD[ROUTED + SHARED : HIDDEN, :] = jnp.zeros((HIDDEN - ROUTED - SHARED, D), BF16)
    H[...] = jnp.zeros(H.shape, BF16)

    def clear(i, carry):
        ACC[i] = jnp.zeros(ACC.shape[1:], F32)
        return carry

    lax.fori_loop(0, 4, clear, 0)
    ASG[...] = jnp.zeros(ASG.shape, F32)
    ASU[...] = jnp.zeros(ASU.shape, F32)

    swap.wait()
    row = lax.broadcasted_iota(jnp.int32, (16, WIDE), 0)
    chunk = jnp.where(row // 8 == c, MINE[c].astype(F32), XR[...].astype(F32)).astype(BF16)
    T[cy, cx, cz, :, pl.ds(pl.multiple_of(c * WIDE, 128), WIDE)] = chunk

    def wide_cols(half, p):
        return pl.ds(pl.multiple_of(half * WIDE + PART_AT[p], 128), T_WIDTH[p])

    def t_cols(half, p):
        return pl.ds(pl.multiple_of(half * WIDE + PART_AT[p], 128), K_WIDTH[p])

    def d_cols(half, p):
        return pl.ds(pl.multiple_of(half * HALF + PART_AT[p], 128), K_WIDTH[p])

    def part_cols(p):
        return pl.ds(PART_AT[p], K_WIDTH[p])

    def place(p, a, b, cc):
        at = [None] * 3
        for dim, i in zip(ORDER[p], (a, b, cc)):
            at[dim] = slice(None) if i is None else i
        return tuple(at)

    def plane(p, cc, j=None):
        at = list(place(p, None, None, cc))
        if j is not None:
            at[min(ORDER[p][:2])] = pl.ds(2 * j, 2)
        return tuple(at)

    def own(p):
        return tuple(here[dim] for dim in ORDER[p])

    def offset(i):
        return (i * (i + 1) // 2) % 4

    def group(p, g):
        return (own(p)[2] + offset(g)) % 4

    def line(p, g, s):
        return place(p, None, (own(p)[1] + offset(s)) % 4, group(p, g)) + (slice(None),)

    parts = range(3)
    steps = (1, 3, 2)
    ROUTE = (0, 1, 1, 0)
    BACK = (2, 1)
    STEP = ((0, 0, 0, 0), (1, 1, 2, 3), (1, 1, 2, 3), (2, 2, 3, 3))

    def arrived(rows, cols, sem):
        at = T.at[rows + (slice(None),) * (4 - len(rows)) + (cols,)]
        send(at, at, sent.at[0], sem, sibling).wait_recv()

    def left(rows, cols, sem):
        at = T.at[rows + (slice(None),) * (4 - len(rows)) + (cols,)]
        send(at, at, sem, sent.at[0], sibling).wait_send()

    wide, narrow = pl.ds(0, WIDE), pl.ds(0, HALF)
    CHUNK, CHUNKS3, LINE = (0, 0, 0), (0, 0, pl.ds(0, 3)), (0, 0)
    LINES3, PLANE, PLANES3 = (0, pl.ds(0, 3)), (0,), (pl.ds(0, 3),)

    def first(p, k):
        at = place(p, *own(p)) + (slice(None), wide_cols(c, p))
        return send(T.at[at], T.at[at], sent.at[0], p1_r.at[k - 1], chip(ORDER[p][0], k))

    def chunk_at(p, g, s, i):
        a, b, _ = own(p)
        return place(p, (a + offset(i)) % 4, (b + offset(s)) % 4, group(p, g)) + (slice(None),)

    def second(p, d, i):
        at = chunk_at(p, 0, 0, i) + (wide_cols(c, p),)
        return send(
            T.at[at], T.at[at], sent.at[1], p2_r.at[d, i], chip(ORDER[p][1], (1, 3)[d])
        )

    def second_relay(p, i):
        d = ROUTE[i]
        at = chunk_at(p, 0, BACK[d], i) + (wide_cols(c, p),)
        return send(T.at[at], T.at[at], sent.at[1], re_r.at[p], chip(ORDER[p][1], (1, 3)[d]))

    def third_chunk(p, d, i):
        at = chunk_at(p, 0, 0, i) + (wide_cols(c, p),)
        return send(
            T.at[at], T.at[at], sent.at[2], p0_r.at[d], chip(ORDER[p][2], (1, 3)[d])
        )

    def third(p, d, s):
        at = line(p, 0, s) + (wide_cols(c, p),)
        return send(
            T.at[at], T.at[at], sent.at[2], p3_r.at[d, s - 1], chip(ORDER[p][2], (1, 3)[d])
        )

    def relay(p, s):
        d = ROUTE[s]
        at = line(p, BACK[d], s) + (wide_cols(c, p),)
        return send(T.at[at], T.at[at], sent.at[2], rl_r.at[s], chip(ORDER[p][2], (1, 3)[d]))

    def share(p, g, s):
        at = line(p, g, s) + (wide_cols(c, p),)
        return send(T.at[at], T.at[at], sent.at[3], sb_r.at[p, STEP[g][s]], sibling)

    for p in parts:
        for k in steps:
            first(p, k).start()
    for p in parts:
        for d in range(2):
            second(p, d, 0).start()
    for p in parts:
        for d in range(2):
            third_chunk(p, d, 0).start()
    for k, i in ((3, 1), (1, 2), (2, 3)):
        arrived(CHUNK, wide, p1_r.at[k - 1])
        for p in parts:
            for d in range(2):
                second(p, d, i).start()
    for p in parts:
        for i in (1, 2, 3):
            for d in range(2):
                third_chunk(p, d, i).start()
        share(p, 0, 0).start()
    for i in range(4):
        for d in range(2):
            arrived(CHUNK, wide, p2_r.at[d, i])
            if ROUTE[i] == d:
                for p in parts:
                    second_relay(p, i).start()
    for s in (1, 2):
        for p in parts:
            for d in range(2):
                third(p, d, s).start()
            share(p, 0, s).start()
    for p in parts:
        arrived(LINE, wide_cols(0, p), re_r.at[p])
        for d in range(2):
            third(p, d, 3).start()
        share(p, 0, 3).start()
    for load in loads:
        load.wait()

    def times(rows, weights):
        weights = weights.reshape(-1, weights.shape[-1])
        return lax.dot_general(rows, weights, (((1,), (1,)), ((), ())), preferred_element_type=F32)

    def pass_on(s):
        for d in range(2):
            arrived(LINE, wide, p0_r.at[d] if s == 0 else p3_r.at[d, s - 1])
            for p in parts:
                if ROUTE[s] == d:
                    relay(p, s).start()
                share(p, BACK[d], s).start()

    def take_in(s):
        arrived(LINE, wide, rl_r.at[s])
        for p in parts:
            share(p, 3, s).start()

    def multiply(m, meanwhile):
        lines = [(g, s) for g in range(4) for s in range(4) if STEP[g][s] == m]

        def turn_step(turn, carry):
            half = (c + turn) % 2

            for p in parts:
                for when, task in meanwhile:
                    if when[1] == p:
                        pl.when(turn == when[0])(task)

                @pl.when(turn == 1)
                def _():
                    arrived(PLANE, wide_cols(0, p), sb_r.at[p, m])

                cols, depth = t_cols(half, p), d_cols(half, p)
                places = [line(p, g, s) for g, s in lines]
                rows = jnp.concatenate([T[at + (cols,)].reshape(64, K_WIDTH[p]) for at in places], axis=0)
                product = times(rows, W[:, :, depth])
                for i, at in enumerate(places):
                    ACC[at + (slice(None),)] += product[64 * i : 64 * i + 64].reshape(4, 16, UP + ROUTED)

                def shared(*places):
                    rows = [T[(cy,) + at + (slice(None), cols)] for at in places]
                    shape = rows[0].shape[:-1]
                    count = 256 // 4 ** (3 - len(shape))
                    rows = jnp.concatenate([v.reshape(count, K_WIDTH[p]) for v in rows], axis=0)
                    gate, up = times(rows, SG[:, depth]), times(rows, SU[:, depth])
                    for i, at in enumerate(places):
                        at = at + (slice(None), slice(None))
                        ASG[at] += gate[count * i : count * i + count].reshape(shape + (SHARED,))
                        ASU[at] += up[count * i : count * i + count].reshape(shape + (SHARED,))

                if ORDER[p][2] == 0:
                    if m == 0:
                        shared((slice(None), slice(None)))
                elif ORDER[p][1] == 0:
                    groups = ((), (0, 1, 2), (3,), ())[m]
                    if groups:
                        shared(*[plane(p, group(p, g))[1:] for g in groups])
                elif m > 0:
                    chunks = [(g, s) for g in range(4) for s in range(4) if max(STEP[g][s], 1) == m]
                    shared(*[line(p, g, s)[1:3] for g, s in chunks])
            return carry

        lax.fori_loop(0, 2, turn_step, 0)

    multiply(0, [((1, 0), lambda: pass_on(0))])
    pass_on(1)
    multiply(1, [((1, 0), lambda: pass_on(2))])
    take_in(0)
    take_in(1)
    multiply(2, [((0, 1), lambda: pass_on(3))])
    take_in(2)
    take_in(3)
    multiply(3, [])
    pl.semaphore_signal(ready, inc=1, device_id=sibling, device_id_type=MESH)

    left(CHUNKS3, wide, sent.at[0])
    left(LINES3, wide, sent.at[1])
    left(PLANES3, wide, sent.at[2])
    left((), wide, sent.at[3])

    expert = f % 16
    gate_lane = lax.broadcasted_iota(jnp.int32, (256, EXTRA), 1)
    chosen = jnp.logical_and(gate_lane % 16 == expert, gate_lane < 48)

    def silu(v):
        return v / (1.0 + jnp.exp(-v))

    def hide(y, carry):
        gates = T[y, :, :, :, HALF:WIDE].reshape(256, EXTRA).astype(F32)
        weight = jnp.sum(jnp.where(chosen, gates, 0.0), axis=1, keepdims=True)
        v = ACC[y, :, :, :, 0:ROUTED].reshape(256, ROUTED)
        u = ACC[y, :, :, :, UP : UP + ROUTED].reshape(256, ROUTED)
        H[y, :, :, :, 0:ROUTED] = (silu(v) * u * weight).astype(BF16).reshape(4, 4, 16, ROUTED)
        return carry

    lax.fori_loop(0, 4, hide, 0)
    mine = (silu(ASG[...]) * ASU[...]).reshape(256, SHARED)
    mine = jnp.concatenate(
        [jnp.zeros((256, ROUTED), F32), mine, jnp.zeros((256, HIDDEN - ROUTED - SHARED), F32)], axis=1
    )
    H[cy] = (H[cy].astype(F32) + mine.reshape(4, 4, 16, HIDDEN)).astype(BF16)

    def landed(p, g, s):
        i = g * 4 + s
        return (
            pl.ds(i % 8 * 4, 4),
            slice(None),
            pl.ds(pl.multiple_of(i // 8 * HALF + PART_AT[p], 128), K_WIDTH[p]),
        )

    def pair(p, g, s):
        at = line(p, g, s) + (t_cols(1 - c, p),)
        sem = pf_r.at[p, s] if g == 3 else pr_r.at[p, g]
        return send(T.at[at], W.at[landed(p, g, s)], sent.at[3], sem, sibling)

    def opposite(p, s):
        at = line(p, 3, s) + (t_cols(c, p),)
        return send(
            T.at[at], RL.at[s, :, :, part_cols(p)], sent.at[2], op_r.at[s],
            chip(ORDER[p][2], (1, 3)[ROUTE[s]]),
        )

    def direct(p, d, s):
        at = line(p, 1 + d, s) + (t_cols(c, p),)
        return send(
            T.at[at], RD.at[d, s, :, :, part_cols(p)], sent.at[2], di_r.at[d, s],
            chip(ORDER[p][2], (1, 3)[d]),
        )

    def back_second(p, s):
        at = line(p, 0, s) + (t_cols(c, p),)
        return send(
            T.at[at], R2.at[s - 1, :, :, part_cols(p)], sent.at[1], q2_r.at[p],
            chip(ORDER[p][1], offset(s)),
        )

    def back_opposite(p, i):
        at = chunk_at(p, 0, 3, i) + (t_cols(c, p),)
        return send(
            T.at[at], RB.at[i, :, part_cols(p)], sent.at[1], qo_r.at[ROUTE[i]],
            chip(ORDER[p][1], (1, 3)[ROUTE[i]]),
        )

    def back_first(p, k):
        a, b, cc = own(p)
        at = place(p, (a + k) % 4, b, cc) + (slice(None), t_cols(c, p))
        return send(
            T.at[at], R3.at[k - 1, :, part_cols(p)], sent.at[0], q3_r.at[p],
            chip(ORDER[p][0], k),
        )

    def down(p, g, half):
        at = plane(p, group(p, g)) + (slice(None), slice(None))
        return jnp.dot(
            H[at].reshape(256, HIDDEN), WD[:, d_cols(half, p)], preferred_element_type=F32
        ).reshape(4, 4, 16, K_WIDTH[p])

    def sum_at(p, *at):
        a, b, _ = own(p)
        i = slice(None) if len(at) == 1 else (a + offset(at[1])) % 4
        at = ((b + offset(at[0])) % 4, i)
        return (at if ORDER[p][1] < ORDER[p][0] else at[::-1]) + (slice(None), part_cols(p))

    far_first = (3, 1, 2, 0)

    def for_sibling(g):
        for p in parts:
            T[plane(p, group(p, g)) + (slice(None), t_cols(1 - c, p))] = down(p, g, 1 - c).astype(BF16)
            for s in far_first:
                pair(p, g, s).start()

    def for_self(p, g, slot):
        SUM[slot, :, :, :, part_cols(p)] = down(p, g, c)

    def add_up(g, slot, s, chosen=parts):
        if g in (1, 2) and ROUTE[s] == g - 1:
            arrived(LINE, narrow, op_r.at[s])
        if g == 0:
            if s in (1, 2):
                arrived((0, 0, pl.ds(0, 2)), narrow, qo_r.at[s - 1])
            for d in range(2):
                arrived(LINE, narrow, di_r.at[d, s])
        for p in chosen:
            if g == 3:
                arrived(LINE, part_cols(p), pf_r.at[p, s])
            elif s == far_first[0]:
                arrived(PLANE, part_cols(p), pr_r.at[p, g])
            if g == 0 and s in (1, 2):
                for i in range(4):
                    if ROUTE[i] == s - 1:
                        SUM[(slot,) + sum_at(p, s, i)] += RB[i, :, part_cols(p)].astype(F32)
            total = SUM[(slot,) + sum_at(p, s)] + W[landed(p, g, s)].astype(F32)
            if g in (1, 2) and ROUTE[s] == g - 1:
                total = total + RL[s, :, :, part_cols(p)].astype(F32)
            if g == 0:
                for d in range(2):
                    total = total + RD[d, s, :, :, part_cols(p)].astype(F32)
                if s == 0:
                    SUM[(slot,) + sum_at(p, s)] = total
                    continue
            T[line(p, g, s) + (t_cols(c, p),)] = total.astype(BF16)
            if g == 3:
                opposite(p, s).start()
            elif g > 0:
                direct(p, g - 1, s).start()
            elif s < 3:
                back_second(p, s).start()
            else:
                for i in range(4):
                    back_opposite(p, i).start()

    pl.semaphore_wait(ready, 1)

    for_sibling(3)
    for p in parts:
        for_self(p, 3, 0)
        for s in far_first:
            add_up(3, 0, s, (p,))
    for g in (2, 1):
        for_sibling(g)
    for g in (2, 1):
        for p in parts:
            for_self(p, g, 2 - g)
    for s in far_first:
        for i in (0, 1) if ROUTE[s] == 0 else (1, 0):
            add_up(2 - i, i, s)
    for_sibling(0)
    for p in parts:
        for_self(p, 0, 0)
    for s in far_first:
        add_up(0, 0, s)

    for p in parts:
        arrived((0, pl.ds(0, 2)), part_cols(p), q2_r.at[p])
        total = SUM[(0,) + sum_at(p, 0)]
        for s in (1, 2):
            total = total + R2[s - 1, :, :, part_cols(p)].astype(F32)
        SUM[(0,) + sum_at(p, 0)] = total
        T[line(p, 0, 0) + (t_cols(c, p),)] = total.astype(BF16)
        for k in steps:
            back_first(p, k).start()
    for p in parts:
        arrived(CHUNKS3, part_cols(p), q3_r.at[p])
        total = SUM[(0,) + sum_at(p, 0, 0)]
        for k in steps:
            total = total + R3[k - 1, :, part_cols(p)].astype(F32)
        FIN[:, part_cols(p)] = total.astype(BF16)
    finish = send(FIN, FR, x_sem.at[2], x_sem.at[3], sibling)
    finish.start()

    def my_rows(v):
        v = v.astype(F32)
        return jnp.where(c == 0, v[0:8], v[8:16]).astype(BF16)

    out[:, pl.ds(pl.multiple_of(c * HALF, 128), HALF)] = my_rows(FIN[...])
    finish.wait_recv()
    out[:, pl.ds(pl.multiple_of((1 - c) * HALF, 128), HALF)] = my_rows(FR[...])

    finish.wait_send()
    left(CHUNKS3, narrow, sent.at[0])
    left(LINES3, narrow, sent.at[1])
    left(PLANES3, narrow, sent.at[2])
    left((), narrow, sent.at[3])


def shards(tok, ids, gv, sg, su, sd, rg, ru, rd):
    def turned(v):
        return jnp.swapaxes(v, -1, -2)

    def blocks(v):
        return turned(v).reshape(1, ROUTED // 16, 16, D)

    arrays = (tok, turned(ids), turned(gv), turned(sg), turned(su), sd, blocks(rg), blocks(ru), rd)
    dma = pltpu.SemaphoreType.DMA
    vmem = pl.BlockSpec(memory_space=pltpu.VMEM)
    hbm = pl.BlockSpec(memory_space=pl.ANY)
    return pl.pallas_call(
        kernel,
        out_shape=jax.ShapeDtypeStruct((8, D), BF16),
        in_specs=[hbm] * 9,
        out_specs=vmem,
        scratch_shapes=[
            pltpu.VMEM((4, 4, 4, 16, 2 * WIDE), BF16),
            pltpu.VMEM(((UP + ROUTED) // 16, 16, D), BF16),
            pltpu.VMEM((SHARED, D), BF16),
            pltpu.VMEM((SHARED, D), BF16),
            pltpu.VMEM((HIDDEN, D), BF16),
            pltpu.VMEM((4, 4, 4, 16, UP + ROUTED), F32),
            pltpu.VMEM((4, 4, 16, SHARED), F32),
            pltpu.VMEM((4, 4, 16, SHARED), F32),
            pltpu.VMEM((4, 4, 4, 16, HIDDEN), BF16),
            pltpu.VMEM((2, 4, 4, 16, HALF), F32),
            pltpu.VMEM((4, 4, 16, HALF), BF16),
            pltpu.VMEM((2, 4, 4, 16, HALF), BF16),
            pltpu.VMEM((2, 4, 16, HALF), BF16),
            pltpu.VMEM((3, 16, HALF), BF16),
            pltpu.VMEM((4, 16, HALF), BF16),
            pltpu.VMEM((8, D), BF16),
            pltpu.VMEM((3, 8), jnp.int32),
            pltpu.VMEM((3, 8), F32),
            pltpu.VMEM((2, 16, WIDE), BF16),
            pltpu.VMEM((16, WIDE), BF16),
            pltpu.VMEM((16, HALF), BF16),
            pltpu.VMEM((16, HALF), BF16),
            dma((6,)), dma((3,)), dma((4,)), dma((4,)),
            dma((3,)), dma((2, 4)), dma((3,)), dma((2,)), dma((2, 3)), dma((4,)), dma((3, 4)),
            dma((3, 3)), dma((3, 4)), dma((4,)), dma((2, 4)), dma((3,)), dma((2,)), dma((3,)),
            pltpu.SemaphoreType.REGULAR,
        ],
        compiler_params=pltpu.CompilerParams(
            collective_id=0, has_side_effects=True, vmem_limit_bytes=62 << 20
        ),
        name="moe_ffn",
    )(*arrays)


def solution(mesh):
    placed = (
        P(("attn", "ffn"), None),
        P(("attn", "ffn"), None),
        P(("attn", "ffn"), None),
        P(None, "ffn"),
        P(None, "ffn"),
        P("ffn", None),
        P("ffn", None, "attn"),
        P("ffn", None, "attn"),
        P("ffn", "attn", None),
    )
    return jax.shard_map(
        shards, mesh=mesh, in_specs=placed, out_specs=P(("attn", "ffn"), None), check_vma=False
    )
```

```python
import jax
import jax.numpy as jnp
from jax import lax
from jax.experimental import pallas as pl
from jax.experimental.pallas import tpu as pltpu
from jax.sharding import PartitionSpec as P

MESH = pl.DeviceIdType.MESH
BF16, F32 = jnp.bfloat16, jnp.float32

D = 7168
HALF = D // 2
EXTRA = 128
WIDE = HALF + EXTRA
PART_AT, T_WIDTH, K_WIDTH = (0, 1280, 2560), (1280, 1280, 1152), (1280, 1280, 1024)
ORDER = ((0, 2, 1), (2, 1, 0), (1, 0, 2))
ROUTED, SHARED, HIDDEN = 320, 160, 512
UP = 384


def kernel(
    tok_hbm, ids_hbm, gv_hbm, sg, su, sd, rg, ru, rd, out,
    T, W, SG, SU, WD, ACC, ASG, ASU, H, SUM, RL, RD, R2, R3, RB, tok, ids, gv, MINE, XR, FIN, FR,
    w_sem, i_sem, x_sem, sent, p1_r, p2_r, re_r, p0_r, p3_r, rl_r, sb_r,
    pr_r, op_r, di_r, q2_r, qo_r, q3_r, ready,
):
    cy = lax.axis_index("attn")
    f = lax.axis_index("ffn")
    cx, cz, c = f // 8, (f // 2) % 4, f % 2
    here = (cy, cx, cz)

    def chip(dim, step):
        at = list(here)
        at[dim] = (at[dim] + step) % 4
        return {"attn": at[0], "ffn": (at[1] * 4 + at[2]) * 2 + c}

    sibling = {"attn": cy, "ffn": f + 1 - 2 * c}

    def send(src, dst, s, r, where):
        return pltpu.make_async_remote_copy(
            src_ref=src, dst_ref=dst, send_sem=s, recv_sem=r, device_id=where, device_id_type=MESH
        )

    inputs = [
        pltpu.make_async_copy(tok_hbm, tok, i_sem.at[0]),
        pltpu.make_async_copy(ids_hbm, ids, i_sem.at[1]),
        pltpu.make_async_copy(gv_hbm, gv, i_sem.at[2]),
    ]
    for copy in inputs:
        copy.start()

    barrier = pltpu.get_barrier_semaphore()
    for dim in range(3):
        for step in (1, 2, 3):
            pl.semaphore_signal(barrier, inc=1, device_id=chip(dim, step), device_id_type=MESH)
    pl.semaphore_signal(barrier, inc=1, device_id=sibling, device_id_type=MESH)

    loads = [
        pltpu.make_async_copy(rg.at[0], W.at[pl.ds(0, ROUTED // 16)], w_sem.at[0]),
        pltpu.make_async_copy(ru.at[0], W.at[pl.ds(UP // 16, ROUTED // 16)], w_sem.at[1]),
        pltpu.make_async_copy(sg, SG, w_sem.at[2]),
        pltpu.make_async_copy(su, SU, w_sem.at[3]),
        pltpu.make_async_copy(rd.at[0], WD.at[pl.ds(0, ROUTED)], w_sem.at[4]),
        pltpu.make_async_copy(sd, WD.at[pl.ds(ROUTED, SHARED)], w_sem.at[5]),
    ]
    for load in loads:
        load.start()
    for copy in inputs:
        copy.wait()

    lane = lax.broadcasted_iota(jnp.int32, (8, EXTRA), 1)
    gate = jnp.zeros((8, EXTRA), F32)
    diagonal = lax.broadcasted_iota(jnp.int32, (8, 8), 0) == lax.broadcasted_iota(jnp.int32, (8, 8), 1)
    expert_lane = (lane % 16).astype(F32)

    def column(v):
        return jnp.sum(jnp.where(diagonal, v, 0.0), axis=1, keepdims=True)

    for j in range(3):
        named = column(ids[j : j + 1, :].astype(F32))
        gate = gate + jnp.where(named == expert_lane, column(gv[j : j + 1, :]), 0.0)
    g_hi = gate.astype(BF16).astype(F32)
    g_mid = (gate - g_hi).astype(BF16).astype(F32)
    g_lo = gate - g_hi - g_mid
    gate = jnp.where(lane < 16, g_hi, jnp.where(lane < 32, g_mid, jnp.where(lane < 48, g_lo, 0.0)))

    def twice(v):
        v = v.astype(F32)
        return jnp.concatenate([v, v], axis=0).astype(BF16)

    for h in range(2):
        MINE[h, :, 0:HALF] = twice(tok[:, h * HALF : (h + 1) * HALF])
        MINE[h, :, HALF:WIDE] = twice(gate)

    pl.semaphore_wait(barrier, 10)
    swap = send(MINE.at[1 - c], XR, x_sem.at[0], x_sem.at[1], sibling)
    swap.start()

    WD[ROUTED + SHARED : HIDDEN, :] = jnp.zeros((HIDDEN - ROUTED - SHARED, D), BF16)
    H[...] = jnp.zeros(H.shape, BF16)

    def clear(i, carry):
        ACC[i] = jnp.zeros(ACC.shape[1:], F32)
        return carry

    lax.fori_loop(0, 4, clear, 0)
    ASG[...] = jnp.zeros(ASG.shape, F32)
    ASU[...] = jnp.zeros(ASU.shape, F32)

    swap.wait()
    row = lax.broadcasted_iota(jnp.int32, (16, WIDE), 0)
    chunk = jnp.where(row // 8 == c, MINE[c].astype(F32), XR[...].astype(F32)).astype(BF16)
    T[cy, cx, cz, :, pl.ds(pl.multiple_of(c * WIDE, 128), WIDE)] = chunk

    def wide_cols(half, p):
        return pl.ds(pl.multiple_of(half * WIDE + PART_AT[p], 128), T_WIDTH[p])

    def t_cols(half, p):
        return pl.ds(pl.multiple_of(half * WIDE + PART_AT[p], 128), K_WIDTH[p])

    def d_cols(half, p):
        return pl.ds(pl.multiple_of(half * HALF + PART_AT[p], 128), K_WIDTH[p])

    def part_cols(p):
        return pl.ds(PART_AT[p], K_WIDTH[p])

    def place(p, a, b, cc):
        at = [None] * 3
        for dim, i in zip(ORDER[p], (a, b, cc)):
            at[dim] = slice(None) if i is None else i
        return tuple(at)

    def plane(p, cc, j=None):
        at = list(place(p, None, None, cc))
        if j is not None:
            at[min(ORDER[p][:2])] = pl.ds(2 * j, 2)
        return tuple(at)

    def own(p):
        return tuple(here[dim] for dim in ORDER[p])

    def offset(i):
        return (i * (i + 1) // 2) % 4

    def group(p, g):
        return (own(p)[2] + offset(g)) % 4

    def line(p, g, s):
        return place(p, None, (own(p)[1] + offset(s)) % 4, group(p, g)) + (slice(None),)

    parts = range(3)
    steps = (1, 3, 2)
    ROUTE = (0, 1, 1, 0)
    BACK = (2, 1)
    STEP = ((0, 0, 0, 0), (1, 1, 2, 3), (1, 1, 2, 3), (2, 2, 3, 3))

    def arrived(rows, cols, sem):
        at = T.at[rows + (slice(None),) * (4 - len(rows)) + (cols,)]
        send(at, at, sent.at[0], sem, sibling).wait_recv()

    def left(rows, cols, sem):
        at = T.at[rows + (slice(None),) * (4 - len(rows)) + (cols,)]
        send(at, at, sem, sent.at[0], sibling).wait_send()

    wide, narrow = pl.ds(0, WIDE), pl.ds(0, HALF)
    CHUNK, CHUNKS3, LINE = (0, 0, 0), (0, 0, pl.ds(0, 3)), (0, 0)
    LINES3, PLANE, PLANES3 = (0, pl.ds(0, 3)), (0,), (pl.ds(0, 3),)

    def first(p, k):
        at = place(p, *own(p)) + (slice(None), wide_cols(c, p))
        return send(T.at[at], T.at[at], sent.at[0], p1_r.at[k - 1], chip(ORDER[p][0], k))

    def chunk_at(p, g, s, i):
        a, b, _ = own(p)
        return place(p, (a + offset(i)) % 4, (b + offset(s)) % 4, group(p, g)) + (slice(None),)

    def second(p, d, i):
        at = chunk_at(p, 0, 0, i) + (wide_cols(c, p),)
        return send(
            T.at[at], T.at[at], sent.at[1], p2_r.at[d, i], chip(ORDER[p][1], (1, 3)[d])
        )

    def second_relay(p, i):
        d = ROUTE[i]
        at = chunk_at(p, 0, BACK[d], i) + (wide_cols(c, p),)
        return send(T.at[at], T.at[at], sent.at[1], re_r.at[p], chip(ORDER[p][1], (1, 3)[d]))

    def third_chunk(p, d, i):
        at = chunk_at(p, 0, 0, i) + (wide_cols(c, p),)
        return send(
            T.at[at], T.at[at], sent.at[2], p0_r.at[d], chip(ORDER[p][2], (1, 3)[d])
        )

    def third(p, d, s):
        at = line(p, 0, s) + (wide_cols(c, p),)
        return send(
            T.at[at], T.at[at], sent.at[2], p3_r.at[d, s - 1], chip(ORDER[p][2], (1, 3)[d])
        )

    def relay(p, s):
        d = ROUTE[s]
        at = line(p, BACK[d], s) + (wide_cols(c, p),)
        return send(T.at[at], T.at[at], sent.at[2], rl_r.at[s], chip(ORDER[p][2], (1, 3)[d]))

    def share(p, g, s):
        at = line(p, g, s) + (wide_cols(c, p),)
        return send(T.at[at], T.at[at], sent.at[3], sb_r.at[p, STEP[g][s]], sibling)

    for p in parts:
        for k in steps:
            first(p, k).start()
    for p in parts:
        for d in range(2):
            second(p, d, 0).start()
    for p in parts:
        for d in range(2):
            third_chunk(p, d, 0).start()
    for k, i in ((3, 1), (1, 2), (2, 3)):
        arrived(CHUNK, wide, p1_r.at[k - 1])
        for p in parts:
            for d in range(2):
                second(p, d, i).start()
    for p in parts:
        for i in (1, 2, 3):
            for d in range(2):
                third_chunk(p, d, i).start()
        share(p, 0, 0).start()
    for i in range(4):
        for d in range(2):
            arrived(CHUNK, wide, p2_r.at[d, i])
            if ROUTE[i] == d:
                for p in parts:
                    second_relay(p, i).start()
    for s in (1, 2):
        for p in parts:
            for d in range(2):
                third(p, d, s).start()
            share(p, 0, s).start()
    for p in parts:
        arrived(LINE, wide_cols(0, p), re_r.at[p])
        for d in range(2):
            third(p, d, 3).start()
        share(p, 0, 3).start()
    for load in loads:
        load.wait()

    def times(rows, weights):
        weights = weights.reshape(-1, weights.shape[-1])
        return lax.dot_general(rows, weights, (((1,), (1,)), ((), ())), preferred_element_type=F32)

    def pass_on(s):
        for d in range(2):
            arrived(LINE, wide, p0_r.at[d] if s == 0 else p3_r.at[d, s - 1])
            for p in parts:
                if ROUTE[s] == d:
                    relay(p, s).start()
                share(p, BACK[d], s).start()

    def take_in(s):
        arrived(LINE, wide, rl_r.at[s])
        for p in parts:
            share(p, 3, s).start()

    def multiply(m, meanwhile):
        lines = [(g, s) for g in range(4) for s in range(4) if STEP[g][s] == m]

        def turn_step(turn, carry):
            half = (c + turn) % 2

            for p in parts:
                for when, task in meanwhile:
                    if when[1] == p:
                        pl.when(turn == when[0])(task)

                @pl.when(turn == 1)
                def _():
                    arrived(PLANE, wide_cols(0, p), sb_r.at[p, m])

                cols, depth = t_cols(half, p), d_cols(half, p)
                places = [line(p, g, s) for g, s in lines]
                rows = jnp.concatenate([T[at + (cols,)].reshape(64, K_WIDTH[p]) for at in places], axis=0)
                product = times(rows, W[:, :, depth])
                for i, at in enumerate(places):
                    ACC[at + (slice(None),)] += product[64 * i : 64 * i + 64].reshape(4, 16, UP + ROUTED)

                def shared(*places):
                    rows = [T[(cy,) + at + (slice(None), cols)] for at in places]
                    shape = rows[0].shape[:-1]
                    count = 256 // 4 ** (3 - len(shape))
                    rows = jnp.concatenate([v.reshape(count, K_WIDTH[p]) for v in rows], axis=0)
                    gate, up = times(rows, SG[:, depth]), times(rows, SU[:, depth])
                    for i, at in enumerate(places):
                        at = at + (slice(None), slice(None))
                        ASG[at] += gate[count * i : count * i + count].reshape(shape + (SHARED,))
                        ASU[at] += up[count * i : count * i + count].reshape(shape + (SHARED,))

                if ORDER[p][2] == 0:
                    if m == 0:
                        shared((slice(None), slice(None)))
                elif ORDER[p][1] == 0:
                    groups = ((), (0, 1, 2), (3,), ())[m]
                    if groups:
                        shared(*[plane(p, group(p, g))[1:] for g in groups])
                elif m > 0:
                    chunks = [(g, s) for g in range(4) for s in range(4) if max(STEP[g][s], 1) == m]
                    shared(*[line(p, g, s)[1:3] for g, s in chunks])
            return carry

        lax.fori_loop(0, 2, turn_step, 0)

    multiply(0, [((1, 0), lambda: pass_on(0))])
    pass_on(1)
    multiply(1, [((1, 0), lambda: pass_on(2))])
    take_in(0)
    take_in(1)
    multiply(2, [((0, 1), lambda: pass_on(3))])
    take_in(2)
    take_in(3)
    multiply(3, [])
    pl.semaphore_signal(ready, inc=1, device_id=sibling, device_id_type=MESH)

    left(CHUNKS3, wide, sent.at[0])
    left(LINES3, wide, sent.at[1])
    left(PLANES3, wide, sent.at[2])
    left((), wide, sent.at[3])

    expert = f % 16
    gate_lane = lax.broadcasted_iota(jnp.int32, (256, EXTRA), 1)
    chosen = jnp.logical_and(gate_lane % 16 == expert, gate_lane < 48)

    def silu(v):
        return v / (1.0 + jnp.exp(-v))

    def hide(y, carry):
        gates = T[y, :, :, :, HALF:WIDE].reshape(256, EXTRA).astype(F32)
        weight = jnp.sum(jnp.where(chosen, gates, 0.0), axis=1, keepdims=True)
        v = ACC[y, :, :, :, 0:ROUTED].reshape(256, ROUTED)
        u = ACC[y, :, :, :, UP : UP + ROUTED].reshape(256, ROUTED)
        H[y, :, :, :, 0:ROUTED] = (silu(v) * u * weight).astype(BF16).reshape(4, 4, 16, ROUTED)
        return carry

    lax.fori_loop(0, 4, hide, 0)
    mine = (silu(ASG[...]) * ASU[...]).reshape(256, SHARED)
    mine = jnp.concatenate(
        [jnp.zeros((256, ROUTED), F32), mine, jnp.zeros((256, HIDDEN - ROUTED - SHARED), F32)], axis=1
    )
    H[cy] = (H[cy].astype(F32) + mine.reshape(4, 4, 16, HIDDEN)).astype(BF16)

    def landed(p, g, s):
        i = g * 4 + s
        return (
            pl.ds(i % 8 * 4, 4),
            slice(None),
            pl.ds(pl.multiple_of(i // 8 * HALF + PART_AT[p], 128), K_WIDTH[p]),
        )

    def pair(p, g, s):
        at = line(p, g, s) + (t_cols(1 - c, p),)
        return send(T.at[at], W.at[landed(p, g, s)], sent.at[3], pr_r.at[p, g, s], sibling)

    def opposite(p, s):
        at = line(p, 3, s) + (t_cols(c, p),)
        return send(
            T.at[at], RL.at[s, :, :, part_cols(p)], sent.at[2], op_r.at[s],
            chip(ORDER[p][2], (1, 3)[ROUTE[s]]),
        )

    def direct(p, d, s):
        at = line(p, 1 + d, s) + (t_cols(c, p),)
        return send(
            T.at[at], RD.at[d, s, :, :, part_cols(p)], sent.at[2], di_r.at[d, s],
            chip(ORDER[p][2], (1, 3)[d]),
        )

    def back_second(p, s):
        at = line(p, 0, s) + (t_cols(c, p),)
        return send(
            T.at[at], R2.at[s - 1, :, :, part_cols(p)], sent.at[1], q2_r.at[p],
            chip(ORDER[p][1], offset(s)),
        )

    def back_opposite(p, i):
        at = chunk_at(p, 0, 3, i) + (t_cols(c, p),)
        return send(
            T.at[at], RB.at[i, :, part_cols(p)], sent.at[1], qo_r.at[ROUTE[i]],
            chip(ORDER[p][1], (1, 3)[ROUTE[i]]),
        )

    def back_first(p, k):
        a, b, cc = own(p)
        at = place(p, (a + k) % 4, b, cc) + (slice(None), t_cols(c, p))
        return send(
            T.at[at], R3.at[k - 1, :, part_cols(p)], sent.at[0], q3_r.at[p],
            chip(ORDER[p][0], k),
        )

    def down(p, g, half):
        at = plane(p, group(p, g)) + (slice(None), slice(None))
        return jnp.dot(
            H[at].reshape(256, HIDDEN), WD[:, d_cols(half, p)], preferred_element_type=F32
        ).reshape(4, 4, 16, K_WIDTH[p])

    def sum_at(p, *at):
        a, b, _ = own(p)
        i = slice(None) if len(at) == 1 else (a + offset(at[1])) % 4
        at = ((b + offset(at[0])) % 4, i)
        return (at if ORDER[p][1] < ORDER[p][0] else at[::-1]) + (slice(None), part_cols(p))

    far_first = (3, 1, 2, 0)

    def for_sibling(*groups):
        for g in groups:
            for p in parts:
                T[plane(p, group(p, g)) + (slice(None), t_cols(1 - c, p))] = down(p, g, 1 - c).astype(BF16)
                pair(p, g, far_first[0]).start()
        for s in far_first[1:]:
            for g in groups:
                for p in parts:
                    pair(p, g, s).start()

    def for_self(p, g, slot):
        SUM[slot, :, :, :, part_cols(p)] = down(p, g, c)

    def add_up(g, slot, s):
        if g in (1, 2) and ROUTE[s] == g - 1:
            arrived(LINE, narrow, op_r.at[s])
        if g == 0:
            if s in (1, 2):
                arrived((0, 0, pl.ds(0, 2)), narrow, qo_r.at[s - 1])
            for d in range(2):
                arrived(LINE, narrow, di_r.at[d, s])
        for p in parts:
            arrived(LINE, part_cols(p), pr_r.at[p, g, s])
            if g == 0 and s in (1, 2):
                for i in range(4):
                    if ROUTE[i] == s - 1:
                        SUM[(slot,) + sum_at(p, s, i)] += RB[i, :, part_cols(p)].astype(F32)
            total = SUM[(slot,) + sum_at(p, s)] + W[landed(p, g, s)].astype(F32)
            if g in (1, 2) and ROUTE[s] == g - 1:
                total = total + RL[s, :, :, part_cols(p)].astype(F32)
            if g == 0:
                for d in range(2):
                    total = total + RD[d, s, :, :, part_cols(p)].astype(F32)
                if s == 0:
                    SUM[(slot,) + sum_at(p, s)] = total
                    continue
            T[line(p, g, s) + (t_cols(c, p),)] = total.astype(BF16)
            if g == 3:
                opposite(p, s).start()
            elif g > 0:
                direct(p, g - 1, s).start()
            elif s < 3:
                back_second(p, s).start()
            else:
                for i in range(4):
                    back_opposite(p, i).start()

    pl.semaphore_wait(ready, 1)

    def middle(s):
        for i in (0, 1) if ROUTE[s] == 0 else (1, 0):
            add_up(2 - i, i, s)

    for_sibling(3)
    for p in parts:
        for_self(p, 3, 0)
    for s in far_first:
        add_up(3, 0, s)
    for_sibling(2, 1)
    for g in (2, 1):
        for p in parts:
            for_self(p, g, 2 - g)
    for s in (3, 1, 2):
        middle(s)
    for_sibling(0)
    for p in parts:
        for_self(p, 0, 2)
    add_up(0, 2, 3)
    middle(0)
    for s in (1, 2, 0):
        add_up(0, 2, s)

    for p in parts:
        arrived((0, pl.ds(0, 2)), part_cols(p), q2_r.at[p])
        total = SUM[(2,) + sum_at(p, 0)]
        for s in (1, 2):
            total = total + R2[s - 1, :, :, part_cols(p)].astype(F32)
        SUM[(2,) + sum_at(p, 0)] = total
        T[line(p, 0, 0) + (t_cols(c, p),)] = total.astype(BF16)
        for k in steps:
            back_first(p, k).start()
    for p in parts:
        arrived(CHUNKS3, part_cols(p), q3_r.at[p])
        total = SUM[(2,) + sum_at(p, 0, 0)]
        for k in steps:
            total = total + R3[k - 1, :, part_cols(p)].astype(F32)
        FIN[:, part_cols(p)] = total.astype(BF16)
    finish = send(FIN, FR, x_sem.at[2], x_sem.at[3], sibling)
    finish.start()

    def my_rows(v):
        v = v.astype(F32)
        return jnp.where(c == 0, v[0:8], v[8:16]).astype(BF16)

    out[:, pl.ds(pl.multiple_of(c * HALF, 128), HALF)] = my_rows(FIN[...])
    finish.wait_recv()
    out[:, pl.ds(pl.multiple_of((1 - c) * HALF, 128), HALF)] = my_rows(FR[...])

    finish.wait_send()
    left(CHUNKS3, narrow, sent.at[0])
    left(LINES3, narrow, sent.at[1])
    left(PLANES3, narrow, sent.at[2])
    left((), narrow, sent.at[3])


def shards(tok, ids, gv, sg, su, sd, rg, ru, rd):
    def turned(v):
        return jnp.swapaxes(v, -1, -2)

    def blocks(v):
        return turned(v).reshape(1, ROUTED // 16, 16, D)

    arrays = (tok, turned(ids), turned(gv), turned(sg), turned(su), sd, blocks(rg), blocks(ru), rd)
    dma = pltpu.SemaphoreType.DMA
    vmem = pl.BlockSpec(memory_space=pltpu.VMEM)
    hbm = pl.BlockSpec(memory_space=pl.ANY)
    return pl.pallas_call(
        kernel,
        out_shape=jax.ShapeDtypeStruct((8, D), BF16),
        in_specs=[hbm] * 9,
        out_specs=vmem,
        scratch_shapes=[
            pltpu.VMEM((4, 4, 4, 16, 2 * WIDE), BF16),
            pltpu.VMEM(((UP + ROUTED) // 16, 16, D), BF16),
            pltpu.VMEM((SHARED, D), BF16),
            pltpu.VMEM((SHARED, D), BF16),
            pltpu.VMEM((HIDDEN, D), BF16),
            pltpu.VMEM((4, 4, 4, 16, UP + ROUTED), F32),
            pltpu.VMEM((4, 4, 16, SHARED), F32),
            pltpu.VMEM((4, 4, 16, SHARED), F32),
            pltpu.VMEM((4, 4, 4, 16, HIDDEN), BF16),
            pltpu.VMEM((3, 4, 4, 16, HALF), F32),
            pltpu.VMEM((4, 4, 16, HALF), BF16),
            pltpu.VMEM((2, 4, 4, 16, HALF), BF16),
            pltpu.VMEM((2, 4, 16, HALF), BF16),
            pltpu.VMEM((3, 16, HALF), BF16),
            pltpu.VMEM((4, 16, HALF), BF16),
            pltpu.VMEM((8, D), BF16),
            pltpu.VMEM((3, 8), jnp.int32),
            pltpu.VMEM((3, 8), F32),
            pltpu.VMEM((2, 16, WIDE), BF16),
            pltpu.VMEM((16, WIDE), BF16),
            pltpu.VMEM((16, HALF), BF16),
            pltpu.VMEM((16, HALF), BF16),
            dma((6,)), dma((3,)), dma((4,)), dma((4,)),
            dma((3,)), dma((2, 4)), dma((3,)), dma((2,)), dma((2, 3)), dma((4,)), dma((3, 4)),
            dma((3, 4, 4)), dma((4,)), dma((2, 4)), dma((3,)), dma((2,)), dma((3,)),
            pltpu.SemaphoreType.REGULAR,
        ],
        compiler_params=pltpu.CompilerParams(
            collective_id=0, has_side_effects=True, vmem_limit_bytes=62 << 20
        ),
        name="moe_ffn",
    )(*arrays)


def solution(mesh):
    placed = (
        P(("attn", "ffn"), None),
        P(("attn", "ffn"), None),
        P(("attn", "ffn"), None),
        P(None, "ffn"),
        P(None, "ffn"),
        P("ffn", None),
        P("ffn", None, "attn"),
        P("ffn", None, "attn"),
        P("ffn", "attn", None),
    )
    return jax.shard_map(
        shards, mesh=mesh, in_specs=placed, out_specs=P(("attn", "ffn"), None), check_vma=False
    )
```

```python
import jax
import jax.numpy as jnp
from jax import lax
from jax.experimental import pallas as pl
from jax.experimental.pallas import tpu as pltpu
from jax.sharding import PartitionSpec as P

MESH = pl.DeviceIdType.MESH
BF16, F32 = jnp.bfloat16, jnp.float32

D = 7168
HALF = D // 2
EXTRA = 128
WIDE = HALF + EXTRA
PART_AT, T_WIDTH, K_WIDTH = (0, 1280, 2560), (1280, 1280, 1152), (1280, 1280, 1024)
ORDER = ((0, 2, 1), (2, 1, 0), (1, 0, 2))
ROUTED, SHARED, HIDDEN = 320, 160, 512
UP = 384


def kernel(
    tok_hbm, ids_hbm, gv_hbm, sg, su, sd, rg, ru, rd, out,
    T, W, SG, SU, WD, ACC, ASG, ASU, H, SUM, RL, RD, R2, R3, RB, tok, ids, gv, MINE, XR, FIN, FR,
    w_sem, i_sem, x_sem, sent, p1_r, p2_r, re_r, p0_r, p3_r, rl_r, sb_r,
    pr_r, op_r, di_r, q2_r, qo_r, q3_r, ready,
):
    cy = lax.axis_index("attn")
    f = lax.axis_index("ffn")
    cx, cz, c = f // 8, (f // 2) % 4, f % 2
    here = (cy, cx, cz)

    def chip(dim, step):
        at = list(here)
        at[dim] = (at[dim] + step) % 4
        return {"attn": at[0], "ffn": (at[1] * 4 + at[2]) * 2 + c}

    sibling = {"attn": cy, "ffn": f + 1 - 2 * c}

    def send(src, dst, s, r, where):
        return pltpu.make_async_remote_copy(
            src_ref=src, dst_ref=dst, send_sem=s, recv_sem=r, device_id=where, device_id_type=MESH
        )

    inputs = [
        pltpu.make_async_copy(tok_hbm, tok, i_sem.at[0]),
        pltpu.make_async_copy(ids_hbm, ids, i_sem.at[1]),
        pltpu.make_async_copy(gv_hbm, gv, i_sem.at[2]),
    ]
    for copy in inputs:
        copy.start()

    barrier = pltpu.get_barrier_semaphore()
    for dim in range(3):
        for step in (1, 2, 3):
            pl.semaphore_signal(barrier, inc=1, device_id=chip(dim, step), device_id_type=MESH)
    pl.semaphore_signal(barrier, inc=1, device_id=sibling, device_id_type=MESH)

    loads = [
        pltpu.make_async_copy(rg.at[0], W.at[pl.ds(0, ROUTED // 16)], w_sem.at[0]),
        pltpu.make_async_copy(ru.at[0], W.at[pl.ds(UP // 16, ROUTED // 16)], w_sem.at[1]),
        pltpu.make_async_copy(sg, SG, w_sem.at[2]),
        pltpu.make_async_copy(su, SU, w_sem.at[3]),
        pltpu.make_async_copy(rd.at[0], WD.at[pl.ds(0, ROUTED)], w_sem.at[4]),
        pltpu.make_async_copy(sd, WD.at[pl.ds(ROUTED, SHARED)], w_sem.at[5]),
    ]
    for load in loads:
        load.start()
    for copy in inputs:
        copy.wait()

    lane = lax.broadcasted_iota(jnp.int32, (8, EXTRA), 1)
    gate = jnp.zeros((8, EXTRA), F32)
    diagonal = lax.broadcasted_iota(jnp.int32, (8, 8), 0) == lax.broadcasted_iota(jnp.int32, (8, 8), 1)
    expert_lane = (lane % 16).astype(F32)

    def column(v):
        return jnp.sum(jnp.where(diagonal, v, 0.0), axis=1, keepdims=True)

    for j in range(3):
        named = column(ids[j : j + 1, :].astype(F32))
        gate = gate + jnp.where(named == expert_lane, column(gv[j : j + 1, :]), 0.0)
    g_hi = gate.astype(BF16).astype(F32)
    g_mid = (gate - g_hi).astype(BF16).astype(F32)
    g_lo = gate - g_hi - g_mid
    gate = jnp.where(lane < 16, g_hi, jnp.where(lane < 32, g_mid, jnp.where(lane < 48, g_lo, 0.0)))

    def twice(v):
        v = v.astype(F32)
        return jnp.concatenate([v, v], axis=0).astype(BF16)

    for h in range(2):
        MINE[h, :, 0:HALF] = twice(tok[:, h * HALF : (h + 1) * HALF])
        MINE[h, :, HALF:WIDE] = twice(gate)

    pl.semaphore_wait(barrier, 10)
    swap = send(MINE.at[1 - c], XR, x_sem.at[0], x_sem.at[1], sibling)
    swap.start()

    WD[ROUTED + SHARED : HIDDEN, :] = jnp.zeros((HIDDEN - ROUTED - SHARED, D), BF16)
    H[...] = jnp.zeros(H.shape, BF16)

    def clear(i, carry):
        ACC[i] = jnp.zeros(ACC.shape[1:], F32)
        return carry

    lax.fori_loop(0, 4, clear, 0)
    ASG[...] = jnp.zeros(ASG.shape, F32)
    ASU[...] = jnp.zeros(ASU.shape, F32)

    swap.wait()
    row = lax.broadcasted_iota(jnp.int32, (16, WIDE), 0)
    chunk = jnp.where(row // 8 == c, MINE[c].astype(F32), XR[...].astype(F32)).astype(BF16)
    T[cy, cx, cz, :, pl.ds(pl.multiple_of(c * WIDE, 128), WIDE)] = chunk

    def wide_cols(half, p):
        return pl.ds(pl.multiple_of(half * WIDE + PART_AT[p], 128), T_WIDTH[p])

    def t_cols(half, p):
        return pl.ds(pl.multiple_of(half * WIDE + PART_AT[p], 128), K_WIDTH[p])

    def d_cols(half, p):
        return pl.ds(pl.multiple_of(half * HALF + PART_AT[p], 128), K_WIDTH[p])

    def part_cols(p):
        return pl.ds(PART_AT[p], K_WIDTH[p])

    def place(p, a, b, cc):
        at = [None] * 3
        for dim, i in zip(ORDER[p], (a, b, cc)):
            at[dim] = slice(None) if i is None else i
        return tuple(at)

    def plane(p, cc, j=None):
        at = list(place(p, None, None, cc))
        if j is not None:
            at[min(ORDER[p][:2])] = pl.ds(2 * j, 2)
        return tuple(at)

    def own(p):
        return tuple(here[dim] for dim in ORDER[p])

    def offset(i):
        return (i * (i + 1) // 2) % 4

    def group(p, g):
        return (own(p)[2] + offset(g)) % 4

    def line(p, g, s):
        return place(p, None, (own(p)[1] + offset(s)) % 4, group(p, g)) + (slice(None),)

    parts = range(3)
    steps = (1, 3, 2)
    ROUTE = (0, 1, 1, 0)
    BACK = (2, 1)
    STEP = ((0, 0, 0, 0), (1, 1, 2, 2), (1, 1, 2, 2), (3, 3, 3, 3))

    def arrived(rows, cols, sem):
        at = T.at[rows + (slice(None),) * (4 - len(rows)) + (cols,)]
        send(at, at, sent.at[0], sem, sibling).wait_recv()

    def left(rows, cols, sem):
        at = T.at[rows + (slice(None),) * (4 - len(rows)) + (cols,)]
        send(at, at, sem, sent.at[0], sibling).wait_send()

    wide, narrow = pl.ds(0, WIDE), pl.ds(0, HALF)
    CHUNK, CHUNKS3, LINE = (0, 0, 0), (0, 0, pl.ds(0, 3)), (0, 0)
    LINES3, PLANE, PLANES3 = (0, pl.ds(0, 3)), (0,), (pl.ds(0, 3),)

    def first(p, k):
        at = place(p, *own(p)) + (slice(None), wide_cols(c, p))
        return send(T.at[at], T.at[at], sent.at[0], p1_r.at[k - 1], chip(ORDER[p][0], k))

    def chunk_at(p, g, s, i):
        a, b, _ = own(p)
        return place(p, (a + offset(i)) % 4, (b + offset(s)) % 4, group(p, g)) + (slice(None),)

    def second(p, d, i):
        at = chunk_at(p, 0, 0, i) + (wide_cols(c, p),)
        return send(
            T.at[at], T.at[at], sent.at[1], p2_r.at[d, i], chip(ORDER[p][1], (1, 3)[d])
        )

    def second_relay(p, i):
        d = ROUTE[i]
        at = chunk_at(p, 0, BACK[d], i) + (wide_cols(c, p),)
        return send(T.at[at], T.at[at], sent.at[1], re_r.at[p], chip(ORDER[p][1], (1, 3)[d]))

    def third_chunk(p, d, i):
        at = chunk_at(p, 0, 0, i) + (wide_cols(c, p),)
        return send(
            T.at[at], T.at[at], sent.at[2], p0_r.at[d], chip(ORDER[p][2], (1, 3)[d])
        )

    def third(p, d, s):
        at = line(p, 0, s) + (wide_cols(c, p),)
        return send(
            T.at[at], T.at[at], sent.at[2], p3_r.at[d, s - 1], chip(ORDER[p][2], (1, 3)[d])
        )

    def relay(p, s):
        d = ROUTE[s]
        at = line(p, BACK[d], s) + (wide_cols(c, p),)
        return send(T.at[at], T.at[at], sent.at[2], rl_r.at[s], chip(ORDER[p][2], (1, 3)[d]))

    def share(p, g, s):
        at = line(p, g, s) + (wide_cols(c, p),)
        return send(T.at[at], T.at[at], sent.at[3], sb_r.at[p, STEP[g][s]], sibling)

    for p in parts:
        for k in steps:
            first(p, k).start()
    for p in parts:
        for d in range(2):
            second(p, d, 0).start()
    for p in parts:
        for d in range(2):
            third_chunk(p, d, 0).start()
    for k, i in ((3, 1), (1, 2), (2, 3)):
        arrived(CHUNK, wide, p1_r.at[k - 1])
        for p in parts:
            for d in range(2):
                second(p, d, i).start()
    for p in parts:
        for i in (1, 2, 3):
            for d in range(2):
                third_chunk(p, d, i).start()
        share(p, 0, 0).start()
    for i in range(4):
        for d in range(2):
            arrived(CHUNK, wide, p2_r.at[d, i])
            if ROUTE[i] == d:
                for p in parts:
                    second_relay(p, i).start()
    for s in (1, 2):
        for p in parts:
            for d in range(2):
                third(p, d, s).start()
            share(p, 0, s).start()
    for p in parts:
        arrived(LINE, wide_cols(0, p), re_r.at[p])
        for d in range(2):
            third(p, d, 3).start()
        share(p, 0, 3).start()
    for load in loads:
        load.wait()

    def times(rows, weights):
        weights = weights.reshape(-1, weights.shape[-1])
        return lax.dot_general(rows, weights, (((1,), (1,)), ((), ())), preferred_element_type=F32)

    def pass_on(s):
        for d in range(2):
            arrived(LINE, wide, p0_r.at[d] if s == 0 else p3_r.at[d, s - 1])
            for p in parts:
                if ROUTE[s] == d:
                    relay(p, s).start()
                share(p, BACK[d], s).start()

    def take_in(s):
        arrived(LINE, wide, rl_r.at[s])
        for p in parts:
            share(p, 3, s).start()

    def multiply(m, meanwhile):
        lines = [(g, s) for g in range(4) for s in range(4) if STEP[g][s] == m]

        def turn_step(turn, carry):
            half = (c + turn) % 2

            for p in parts:
                for when, task in meanwhile:
                    if when[1] == p:
                        pl.when(turn == when[0])(task)

                @pl.when(turn == 1)
                def _():
                    arrived(PLANE, wide_cols(0, p), sb_r.at[p, m])

                cols, depth = t_cols(half, p), d_cols(half, p)
                places = [line(p, g, s) for g, s in lines]
                rows = jnp.concatenate([T[at + (cols,)].reshape(64, K_WIDTH[p]) for at in places], axis=0)
                product = times(rows, W[:, :, depth])
                for i, at in enumerate(places):
                    ACC[at + (slice(None),)] += product[64 * i : 64 * i + 64].reshape(4, 16, UP + ROUTED)

                def shared(*places):
                    rows = [T[(cy,) + at + (slice(None), cols)] for at in places]
                    shape = rows[0].shape[:-1]
                    count = 256 // 4 ** (3 - len(shape))
                    rows = jnp.concatenate([v.reshape(count, K_WIDTH[p]) for v in rows], axis=0)
                    gate, up = times(rows, SG[:, depth]), times(rows, SU[:, depth])
                    for i, at in enumerate(places):
                        at = at + (slice(None), slice(None))
                        ASG[at] += gate[count * i : count * i + count].reshape(shape + (SHARED,))
                        ASU[at] += up[count * i : count * i + count].reshape(shape + (SHARED,))

                if ORDER[p][2] == 0:
                    if m == 0:
                        shared((slice(None), slice(None)))
                elif ORDER[p][1] == 0:
                    groups = ((), (0, 1, 2), (), (3,))[m]
                    if groups:
                        shared(*[plane(p, group(p, g))[1:] for g in groups])
                elif m > 0:
                    chunks = [(g, s) for g in range(4) for s in range(4) if max(STEP[g][s], 1) == m]
                    shared(*[line(p, g, s)[1:3] for g, s in chunks])
            return carry

        lax.fori_loop(0, 2, turn_step, 0)

    multiply(0, [((1, 0), lambda: pass_on(0))])
    pass_on(1)
    multiply(1, [((1, 0), lambda: pass_on(2))])
    pass_on(3)
    multiply(2, [((1, 0), lambda: take_in(0)), ((1, 2), lambda: take_in(1))])
    take_in(2)
    take_in(3)
    multiply(3, [])
    pl.semaphore_signal(ready, inc=1, device_id=sibling, device_id_type=MESH)

    left(CHUNKS3, wide, sent.at[0])
    left(LINES3, wide, sent.at[1])
    left(PLANES3, wide, sent.at[2])
    left((), wide, sent.at[3])

    expert = f % 16
    gate_lane = lax.broadcasted_iota(jnp.int32, (256, EXTRA), 1)
    chosen = jnp.logical_and(gate_lane % 16 == expert, gate_lane < 48)

    def silu(v):
        return v / (1.0 + jnp.exp(-v))

    def hide(y, carry):
        gates = T[y, :, :, :, HALF:WIDE].reshape(256, EXTRA).astype(F32)
        weight = jnp.sum(jnp.where(chosen, gates, 0.0), axis=1, keepdims=True)
        v = ACC[y, :, :, :, 0:ROUTED].reshape(256, ROUTED)
        u = ACC[y, :, :, :, UP : UP + ROUTED].reshape(256, ROUTED)
        H[y, :, :, :, 0:ROUTED] = (silu(v) * u * weight).astype(BF16).reshape(4, 4, 16, ROUTED)
        return carry

    lax.fori_loop(0, 4, hide, 0)
    mine = (silu(ASG[...]) * ASU[...]).reshape(256, SHARED)
    mine = jnp.concatenate(
        [jnp.zeros((256, ROUTED), F32), mine, jnp.zeros((256, HIDDEN - ROUTED - SHARED), F32)], axis=1
    )
    H[cy] = (H[cy].astype(F32) + mine.reshape(4, 4, 16, HIDDEN)).astype(BF16)

    def landed(p, g, s):
        i = g * 4 + s
        return (
            pl.ds(i % 8 * 4, 4),
            slice(None),
            pl.ds(pl.multiple_of(i // 8 * HALF + PART_AT[p], 128), K_WIDTH[p]),
        )

    def pair(p, g, s):
        at = line(p, g, s) + (t_cols(1 - c, p),)
        return send(T.at[at], W.at[landed(p, g, s)], sent.at[3], pr_r.at[p, g, s], sibling)

    def opposite(p, s):
        at = line(p, 3, s) + (t_cols(c, p),)
        return send(
            T.at[at], RL.at[s, :, :, part_cols(p)], sent.at[2], op_r.at[s],
            chip(ORDER[p][2], (1, 3)[ROUTE[s]]),
        )

    def direct(p, d, s):
        at = line(p, 1 + d, s) + (t_cols(c, p),)
        return send(
            T.at[at], RD.at[d, s, :, :, part_cols(p)], sent.at[2], di_r.at[d, s],
            chip(ORDER[p][2], (1, 3)[d]),
        )

    def back_second(p, s):
        at = line(p, 0, s) + (t_cols(c, p),)
        return send(
            T.at[at], R2.at[s - 1, :, :, part_cols(p)], sent.at[1], q2_r.at[p],
            chip(ORDER[p][1], offset(s)),
        )

    def back_opposite(p, i):
        at = chunk_at(p, 0, 3, i) + (t_cols(c, p),)
        return send(
            T.at[at], RB.at[i, :, part_cols(p)], sent.at[1], qo_r.at[ROUTE[i]],
            chip(ORDER[p][1], (1, 3)[ROUTE[i]]),
        )

    def back_first(p, k):
        a, b, cc = own(p)
        at = place(p, (a + k) % 4, b, cc) + (slice(None), t_cols(c, p))
        return send(
            T.at[at], R3.at[k - 1, :, part_cols(p)], sent.at[0], q3_r.at[p],
            chip(ORDER[p][0], k),
        )

    def down(p, g, half):
        at = plane(p, group(p, g)) + (slice(None), slice(None))
        return jnp.dot(
            H[at].reshape(256, HIDDEN), WD[:, d_cols(half, p)], preferred_element_type=F32
        ).reshape(4, 4, 16, K_WIDTH[p])

    def sum_at(p, *at):
        a, b, _ = own(p)
        i = slice(None) if len(at) == 1 else (a + offset(at[1])) % 4
        at = ((b + offset(at[0])) % 4, i)
        return (at if ORDER[p][1] < ORDER[p][0] else at[::-1]) + (slice(None), part_cols(p))

    far_first = (3, 1, 2, 0)

    def for_sibling(*groups):
        for g in groups:
            for p in parts:
                T[plane(p, group(p, g)) + (slice(None), t_cols(1 - c, p))] = down(p, g, 1 - c).astype(BF16)
                pair(p, g, far_first[0]).start()
        for s in far_first[1:]:
            for g in groups:
                for p in parts:
                    pair(p, g, s).start()

    def for_self(p, g, slot):
        SUM[slot, :, :, :, part_cols(p)] = down(p, g, c)

    def add_up(g, slot, s):
        if g in (1, 2) and ROUTE[s] == g - 1:
            arrived(LINE, narrow, op_r.at[s])
        if g == 0:
            if s in (1, 2):
                arrived((0, 0, pl.ds(0, 2)), narrow, qo_r.at[s - 1])
            for d in range(2):
                arrived(LINE, narrow, di_r.at[d, s])
        for p in parts:
            arrived(LINE, part_cols(p), pr_r.at[p, g, s])
            if g == 0 and s in (1, 2):
                for i in range(4):
                    if ROUTE[i] == s - 1:
                        SUM[(slot,) + sum_at(p, s, i)] += RB[i, :, part_cols(p)].astype(F32)
            total = SUM[(slot,) + sum_at(p, s)] + W[landed(p, g, s)].astype(F32)
            if g in (1, 2) and ROUTE[s] == g - 1:
                total = total + RL[s, :, :, part_cols(p)].astype(F32)
            if g == 0:
                for d in range(2):
                    total = total + RD[d, s, :, :, part_cols(p)].astype(F32)
                if s == 0:
                    SUM[(slot,) + sum_at(p, s)] = total
                    continue
            T[line(p, g, s) + (t_cols(c, p),)] = total.astype(BF16)
            if g == 3:
                opposite(p, s).start()
            elif g > 0:
                direct(p, g - 1, s).start()
            elif s < 3:
                back_second(p, s).start()
            else:
                for i in range(4):
                    back_opposite(p, i).start()

    pl.semaphore_wait(ready, 1)

    def middle(s):
        for i in (0, 1) if ROUTE[s] == 0 else (1, 0):
            add_up(2 - i, i, s)

    for_sibling(3)
    for p in parts:
        for_self(p, 3, 0)
    for s in far_first:
        add_up(3, 0, s)
    for_sibling(2, 1)
    for g in (2, 1):
        for p in parts:
            for_self(p, g, 2 - g)
    for s in (3, 1, 2):
        middle(s)
    for_sibling(0)
    for p in parts:
        for_self(p, 0, 2)
    add_up(0, 2, 3)
    middle(0)
    for s in (1, 2, 0):
        add_up(0, 2, s)

    for p in parts:
        arrived((0, pl.ds(0, 2)), part_cols(p), q2_r.at[p])
        total = SUM[(2,) + sum_at(p, 0)]
        for s in (1, 2):
            total = total + R2[s - 1, :, :, part_cols(p)].astype(F32)
        SUM[(2,) + sum_at(p, 0)] = total
        T[line(p, 0, 0) + (t_cols(c, p),)] = total.astype(BF16)
        for k in steps:
            back_first(p, k).start()
    for p in parts:
        arrived(CHUNKS3, part_cols(p), q3_r.at[p])
        total = SUM[(2,) + sum_at(p, 0, 0)]
        for k in steps:
            total = total + R3[k - 1, :, part_cols(p)].astype(F32)
        FIN[:, part_cols(p)] = total.astype(BF16)
    finish = send(FIN, FR, x_sem.at[2], x_sem.at[3], sibling)
    finish.start()

    def my_rows(v):
        v = v.astype(F32)
        return jnp.where(c == 0, v[0:8], v[8:16]).astype(BF16)

    out[:, pl.ds(pl.multiple_of(c * HALF, 128), HALF)] = my_rows(FIN[...])
    finish.wait_recv()
    out[:, pl.ds(pl.multiple_of((1 - c) * HALF, 128), HALF)] = my_rows(FR[...])

    finish.wait_send()
    left(CHUNKS3, narrow, sent.at[0])
    left(LINES3, narrow, sent.at[1])
    left(PLANES3, narrow, sent.at[2])
    left((), narrow, sent.at[3])


def shards(tok, ids, gv, sg, su, sd, rg, ru, rd):
    def turned(v):
        return jnp.swapaxes(v, -1, -2)

    def blocks(v):
        return turned(v).reshape(1, ROUTED // 16, 16, D)

    arrays = (tok, turned(ids), turned(gv), turned(sg), turned(su), sd, blocks(rg), blocks(ru), rd)
    dma = pltpu.SemaphoreType.DMA
    vmem = pl.BlockSpec(memory_space=pltpu.VMEM)
    hbm = pl.BlockSpec(memory_space=pl.ANY)
    return pl.pallas_call(
        kernel,
        out_shape=jax.ShapeDtypeStruct((8, D), BF16),
        in_specs=[hbm] * 9,
        out_specs=vmem,
        scratch_shapes=[
            pltpu.VMEM((4, 4, 4, 16, 2 * WIDE), BF16),
            pltpu.VMEM(((UP + ROUTED) // 16, 16, D), BF16),
            pltpu.VMEM((SHARED, D), BF16),
            pltpu.VMEM((SHARED, D), BF16),
            pltpu.VMEM((HIDDEN, D), BF16),
            pltpu.VMEM((4, 4, 4, 16, UP + ROUTED), F32),
            pltpu.VMEM((4, 4, 16, SHARED), F32),
            pltpu.VMEM((4, 4, 16, SHARED), F32),
            pltpu.VMEM((4, 4, 4, 16, HIDDEN), BF16),
            pltpu.VMEM((3, 4, 4, 16, HALF), F32),
            pltpu.VMEM((4, 4, 16, HALF), BF16),
            pltpu.VMEM((2, 4, 4, 16, HALF), BF16),
            pltpu.VMEM((2, 4, 16, HALF), BF16),
            pltpu.VMEM((3, 16, HALF), BF16),
            pltpu.VMEM((4, 16, HALF), BF16),
            pltpu.VMEM((8, D), BF16),
            pltpu.VMEM((3, 8), jnp.int32),
            pltpu.VMEM((3, 8), F32),
            pltpu.VMEM((2, 16, WIDE), BF16),
            pltpu.VMEM((16, WIDE), BF16),
            pltpu.VMEM((16, HALF), BF16),
            pltpu.VMEM((16, HALF), BF16),
            dma((6,)), dma((3,)), dma((4,)), dma((4,)),
            dma((3,)), dma((2, 4)), dma((3,)), dma((2,)), dma((2, 3)), dma((4,)), dma((3, 4)),
            dma((3, 4, 4)), dma((4,)), dma((2, 4)), dma((3,)), dma((2,)), dma((3,)),
            pltpu.SemaphoreType.REGULAR,
        ],
        compiler_params=pltpu.CompilerParams(
            collective_id=0, has_side_effects=True, vmem_limit_bytes=62 << 20
        ),
        name="moe_ffn",
    )(*arrays)


def solution(mesh):
    placed = (
        P(("attn", "ffn"), None),
        P(("attn", "ffn"), None),
        P(("attn", "ffn"), None),
        P(None, "ffn"),
        P(None, "ffn"),
        P("ffn", None),
        P("ffn", None, "attn"),
        P("ffn", None, "attn"),
        P("ffn", "attn", None),
    )
    return jax.shard_map(
        shards, mesh=mesh, in_specs=placed, out_specs=P(("attn", "ffn"), None), check_vma=False
    )
```

```python
import jax
import jax.numpy as jnp
from jax import lax
from jax.experimental import pallas as pl
from jax.experimental.pallas import tpu as pltpu
from jax.sharding import PartitionSpec as P

MESH = pl.DeviceIdType.MESH
BF16, F32 = jnp.bfloat16, jnp.float32

D = 7168
HALF = D // 2
EXTRA = 128
WIDE = HALF + EXTRA
PART_AT, T_WIDTH, K_WIDTH = (0, 1280, 2560), (1280, 1280, 1152), (1280, 1280, 1024)
ORDER = ((0, 2, 1), (2, 1, 0), (1, 0, 2))
ROUTED, SHARED, HIDDEN = 320, 160, 512
UP = 384


def kernel(
    tok_hbm, ids_hbm, gv_hbm, sg, su, sd, rg, ru, rd, out,
    T, W, SG, SU, WD, ACC, ASG, ASU, H, SUM, RL, RD, R2, R3, RB, tok, ids, gv, MINE, XR, FIN, FR,
    w_sem, i_sem, x_sem, sent, p1_r, p2_r, re_r, p0_r, p3_r, rl_r, sb_r,
    pr_r, op_r, di_r, q2_r, qo_r, q3_r, ready,
):
    cy = lax.axis_index("attn")
    f = lax.axis_index("ffn")
    cx, cz, c = f // 8, (f // 2) % 4, f % 2
    here = (cy, cx, cz)

    def chip(dim, step):
        at = list(here)
        at[dim] = (at[dim] + step) % 4
        return {"attn": at[0], "ffn": (at[1] * 4 + at[2]) * 2 + c}

    sibling = {"attn": cy, "ffn": f + 1 - 2 * c}

    def send(src, dst, s, r, where):
        return pltpu.make_async_remote_copy(
            src_ref=src, dst_ref=dst, send_sem=s, recv_sem=r, device_id=where, device_id_type=MESH
        )

    inputs = [
        pltpu.make_async_copy(tok_hbm, tok, i_sem.at[0]),
        pltpu.make_async_copy(ids_hbm, ids, i_sem.at[1]),
        pltpu.make_async_copy(gv_hbm, gv, i_sem.at[2]),
    ]
    for copy in inputs:
        copy.start()

    barrier = pltpu.get_barrier_semaphore()
    for dim in range(3):
        for step in (1, 2, 3):
            pl.semaphore_signal(barrier, inc=1, device_id=chip(dim, step), device_id_type=MESH)
    pl.semaphore_signal(barrier, inc=1, device_id=sibling, device_id_type=MESH)

    loads = [
        pltpu.make_async_copy(rg.at[0], W.at[pl.ds(0, ROUTED // 16)], w_sem.at[0]),
        pltpu.make_async_copy(ru.at[0], W.at[pl.ds(UP // 16, ROUTED // 16)], w_sem.at[1]),
        pltpu.make_async_copy(sg, SG, w_sem.at[2]),
        pltpu.make_async_copy(su, SU, w_sem.at[3]),
        pltpu.make_async_copy(rd.at[0], WD.at[pl.ds(0, ROUTED)], w_sem.at[4]),
        pltpu.make_async_copy(sd, WD.at[pl.ds(ROUTED, SHARED)], w_sem.at[5]),
    ]
    for load in loads:
        load.start()
    for copy in inputs:
        copy.wait()

    lane = lax.broadcasted_iota(jnp.int32, (8, EXTRA), 1)
    gate = jnp.zeros((8, EXTRA), F32)
    diagonal = lax.broadcasted_iota(jnp.int32, (8, 8), 0) == lax.broadcasted_iota(jnp.int32, (8, 8), 1)
    expert_lane = (lane % 16).astype(F32)

    def column(v):
        return jnp.sum(jnp.where(diagonal, v, 0.0), axis=1, keepdims=True)

    for j in range(3):
        named = column(ids[j : j + 1, :].astype(F32))
        gate = gate + jnp.where(named == expert_lane, column(gv[j : j + 1, :]), 0.0)
    g_hi = gate.astype(BF16).astype(F32)
    g_mid = (gate - g_hi).astype(BF16).astype(F32)
    g_lo = gate - g_hi - g_mid
    gate = jnp.where(lane < 16, g_hi, jnp.where(lane < 32, g_mid, jnp.where(lane < 48, g_lo, 0.0)))

    def twice(v):
        v = v.astype(F32)
        return jnp.concatenate([v, v], axis=0).astype(BF16)

    for h in range(2):
        MINE[h, :, 0:HALF] = twice(tok[:, h * HALF : (h + 1) * HALF])
        MINE[h, :, HALF:WIDE] = twice(gate)

    pl.semaphore_wait(barrier, 10)
    swap = send(MINE.at[1 - c], XR, x_sem.at[0], x_sem.at[1], sibling)
    swap.start()

    WD[ROUTED + SHARED : HIDDEN, :] = jnp.zeros((HIDDEN - ROUTED - SHARED, D), BF16)
    H[...] = jnp.zeros(H.shape, BF16)

    def clear(i, carry):
        ACC[i] = jnp.zeros(ACC.shape[1:], F32)
        return carry

    lax.fori_loop(0, 4, clear, 0)
    ASG[...] = jnp.zeros(ASG.shape, F32)
    ASU[...] = jnp.zeros(ASU.shape, F32)

    swap.wait()
    row = lax.broadcasted_iota(jnp.int32, (16, WIDE), 0)
    chunk = jnp.where(row // 8 == c, MINE[c].astype(F32), XR[...].astype(F32)).astype(BF16)
    T[cy, cx, cz, :, pl.ds(pl.multiple_of(c * WIDE, 128), WIDE)] = chunk

    def wide_cols(half, p):
        return pl.ds(pl.multiple_of(half * WIDE + PART_AT[p], 128), T_WIDTH[p])

    def t_cols(half, p):
        return pl.ds(pl.multiple_of(half * WIDE + PART_AT[p], 128), K_WIDTH[p])

    def d_cols(half, p):
        return pl.ds(pl.multiple_of(half * HALF + PART_AT[p], 128), K_WIDTH[p])

    def part_cols(p):
        return pl.ds(PART_AT[p], K_WIDTH[p])

    def place(p, a, b, cc):
        at = [None] * 3
        for dim, i in zip(ORDER[p], (a, b, cc)):
            at[dim] = slice(None) if i is None else i
        return tuple(at)

    def plane(p, cc, j=None):
        at = list(place(p, None, None, cc))
        if j is not None:
            at[min(ORDER[p][:2])] = pl.ds(2 * j, 2)
        return tuple(at)

    def own(p):
        return tuple(here[dim] for dim in ORDER[p])

    def offset(i):
        return (i * (i + 1) // 2) % 4

    def group(p, g):
        return (own(p)[2] + offset(g)) % 4

    def line(p, g, s):
        return place(p, None, (own(p)[1] + offset(s)) % 4, group(p, g)) + (slice(None),)

    parts = range(3)
    steps = (1, 3, 2)
    ROUTE = (0, 1, 1, 0)
    BACK = (2, 1)
    STEP = ((0, 0, 0, 0), (1, 1, 2, 2), (1, 1, 2, 2), (3, 3, 3, 3))

    def arrived(rows, cols, sem):
        at = T.at[rows + (slice(None),) * (4 - len(rows)) + (cols,)]
        send(at, at, sent.at[0], sem, sibling).wait_recv()

    def left(rows, cols, sem):
        at = T.at[rows + (slice(None),) * (4 - len(rows)) + (cols,)]
        send(at, at, sem, sent.at[0], sibling).wait_send()

    wide, narrow = pl.ds(0, WIDE), pl.ds(0, HALF)
    CHUNK, CHUNKS3, LINE = (0, 0, 0), (0, 0, pl.ds(0, 3)), (0, 0)
    LINES3, PLANE, PLANES3 = (0, pl.ds(0, 3)), (0,), (pl.ds(0, 3),)

    def first(p, k):
        at = place(p, *own(p)) + (slice(None), wide_cols(c, p))
        return send(T.at[at], T.at[at], sent.at[0], p1_r.at[k - 1], chip(ORDER[p][0], k))

    def chunk_at(p, g, s, i):
        a, b, _ = own(p)
        return place(p, (a + offset(i)) % 4, (b + offset(s)) % 4, group(p, g)) + (slice(None),)

    def second(p, d, i):
        at = chunk_at(p, 0, 0, i) + (wide_cols(c, p),)
        return send(
            T.at[at], T.at[at], sent.at[1], p2_r.at[d, i], chip(ORDER[p][1], (1, 3)[d])
        )

    def second_relay(p, i):
        d = ROUTE[i]
        at = chunk_at(p, 0, BACK[d], i) + (wide_cols(c, p),)
        return send(T.at[at], T.at[at], sent.at[1], re_r.at[p], chip(ORDER[p][1], (1, 3)[d]))

    def third_chunk(p, d, i):
        at = chunk_at(p, 0, 0, i) + (wide_cols(c, p),)
        return send(
            T.at[at], T.at[at], sent.at[2], p0_r.at[d], chip(ORDER[p][2], (1, 3)[d])
        )

    def third(p, d, s):
        at = line(p, 0, s) + (wide_cols(c, p),)
        return send(
            T.at[at], T.at[at], sent.at[2], p3_r.at[d, s - 1], chip(ORDER[p][2], (1, 3)[d])
        )

    def relay(p, s):
        d = ROUTE[s]
        at = line(p, BACK[d], s) + (wide_cols(c, p),)
        return send(T.at[at], T.at[at], sent.at[2], rl_r.at[s], chip(ORDER[p][2], (1, 3)[d]))

    def share(p, g, s):
        at = line(p, g, s) + (wide_cols(c, p),)
        return send(T.at[at], T.at[at], sent.at[3], sb_r.at[p, STEP[g][s]], sibling)

    for p in parts:
        for k in steps:
            first(p, k).start()
    for p in parts:
        for d in range(2):
            second(p, d, 0).start()
    for p in parts:
        for d in range(2):
            third_chunk(p, d, 0).start()
    for k, i in ((3, 1), (1, 2), (2, 3)):
        arrived(CHUNK, wide, p1_r.at[k - 1])
        for p in parts:
            for d in range(2):
                second(p, d, i).start()
    for p in parts:
        for i in (1, 2, 3):
            for d in range(2):
                third_chunk(p, d, i).start()
        share(p, 0, 0).start()
    for i in range(4):
        for d in range(2):
            arrived(CHUNK, wide, p2_r.at[d, i])
            if ROUTE[i] == d:
                for p in parts:
                    second_relay(p, i).start()
    for s in (1, 2):
        for p in parts:
            for d in range(2):
                third(p, d, s).start()
            share(p, 0, s).start()
    for p in parts:
        arrived(LINE, wide_cols(0, p), re_r.at[p])
        for d in range(2):
            third(p, d, 3).start()
        share(p, 0, 3).start()
    for load in loads:
        load.wait()

    def times(rows, weights):
        weights = weights.reshape(-1, weights.shape[-1])
        return lax.dot_general(rows, weights, (((1,), (1,)), ((), ())), preferred_element_type=F32)

    def pass_on(s):
        for d in range(2):
            arrived(LINE, wide, p0_r.at[d] if s == 0 else p3_r.at[d, s - 1])
            for p in parts:
                if ROUTE[s] == d:
                    relay(p, s).start()
                share(p, BACK[d], s).start()

    def take_in(s):
        arrived(LINE, wide, rl_r.at[s])
        for p in parts:
            share(p, 3, s).start()

    def multiply(m, meanwhile):
        lines = [(g, s) for g in range(4) for s in range(4) if STEP[g][s] == m]

        def turn_step(turn, carry):
            half = (c + turn) % 2

            for p in parts:
                for when, task in meanwhile:
                    if when[1] == p:
                        pl.when(turn == when[0])(task)

                @pl.when(turn == 1)
                def _():
                    arrived(PLANE, wide_cols(0, p), sb_r.at[p, m])

                cols, depth = t_cols(half, p), d_cols(half, p)
                places = [line(p, g, s) for g, s in lines]
                rows = jnp.concatenate([T[at + (cols,)].reshape(64, K_WIDTH[p]) for at in places], axis=0)
                product = times(rows, W[:, :, depth])
                for i, at in enumerate(places):
                    ACC[at + (slice(None),)] += product[64 * i : 64 * i + 64].reshape(4, 16, UP + ROUTED)

                def shared(*places):
                    rows = [T[(cy,) + at + (slice(None), cols)] for at in places]
                    shape = rows[0].shape[:-1]
                    count = 256 // 4 ** (3 - len(shape))
                    rows = jnp.concatenate([v.reshape(count, K_WIDTH[p]) for v in rows], axis=0)
                    gate, up = times(rows, SG[:, depth]), times(rows, SU[:, depth])
                    for i, at in enumerate(places):
                        at = at + (slice(None), slice(None))
                        ASG[at] += gate[count * i : count * i + count].reshape(shape + (SHARED,))
                        ASU[at] += up[count * i : count * i + count].reshape(shape + (SHARED,))

                if ORDER[p][2] == 0:
                    if m == 0:
                        shared((slice(None), slice(None)))
                elif ORDER[p][1] == 0:
                    groups = ((), (0, 1, 2), (), (3,))[m]
                    if groups:
                        shared(*[plane(p, group(p, g))[1:] for g in groups])
                elif m > 0:
                    chunks = [(g, s) for g in range(4) for s in range(4) if max(STEP[g][s], 1) == m]
                    shared(*[line(p, g, s)[1:3] for g, s in chunks])
            return carry

        lax.fori_loop(0, 2, turn_step, 0)

    multiply(0, [((1, 0), lambda: pass_on(0))])
    pass_on(1)
    multiply(1, [((1, 0), lambda: pass_on(2))])
    pass_on(3)
    multiply(2, [((0, 2), lambda: take_in(0)), ((1, 0), lambda: take_in(1)), ((1, 2), lambda: take_in(2))])
    take_in(3)
    multiply(3, [])
    pl.semaphore_signal(ready, inc=1, device_id=sibling, device_id_type=MESH)

    expert = f % 16
    gate_lane = lax.broadcasted_iota(jnp.int32, (256, EXTRA), 1)
    chosen = jnp.logical_and(gate_lane % 16 == expert, gate_lane < 48)

    def silu(v):
        return v / (1.0 + jnp.exp(-v))

    def hide(y, carry):
        gates = T[y, :, :, :, HALF:WIDE].reshape(256, EXTRA).astype(F32)
        weight = jnp.sum(jnp.where(chosen, gates, 0.0), axis=1, keepdims=True)
        v = ACC[y, :, :, :, 0:ROUTED].reshape(256, ROUTED)
        u = ACC[y, :, :, :, UP : UP + ROUTED].reshape(256, ROUTED)
        H[y, :, :, :, 0:ROUTED] = (silu(v) * u * weight).astype(BF16).reshape(4, 4, 16, ROUTED)
        return carry

    lax.fori_loop(0, 4, hide, 0)
    mine = (silu(ASG[...]) * ASU[...]).reshape(256, SHARED)
    mine = jnp.concatenate(
        [jnp.zeros((256, ROUTED), F32), mine, jnp.zeros((256, HIDDEN - ROUTED - SHARED), F32)], axis=1
    )
    H[cy] = (H[cy].astype(F32) + mine.reshape(4, 4, 16, HIDDEN)).astype(BF16)

    def landed(p, g, s):
        i = g * 4 + s
        return (
            pl.ds(i % 8 * 4, 4),
            slice(None),
            pl.ds(pl.multiple_of(i // 8 * HALF + PART_AT[p], 128), K_WIDTH[p]),
        )

    def pair(p, g, s):
        at = line(p, g, s) + (t_cols(1 - c, p),)
        return send(T.at[at], W.at[landed(p, g, s)], sent.at[3], pr_r.at[p, g, s], sibling)

    def opposite(p, s):
        at = line(p, 3, s) + (t_cols(c, p),)
        return send(
            T.at[at], RL.at[s, :, :, part_cols(p)], sent.at[2], op_r.at[s],
            chip(ORDER[p][2], (1, 3)[ROUTE[s]]),
        )

    def direct(p, d, s):
        at = line(p, 1 + d, s) + (t_cols(c, p),)
        return send(
            T.at[at], RD.at[d, s, :, :, part_cols(p)], sent.at[2], di_r.at[d, s],
            chip(ORDER[p][2], (1, 3)[d]),
        )

    def back_second(p, s):
        at = line(p, 0, s) + (t_cols(c, p),)
        return send(
            T.at[at], R2.at[s - 1, :, :, part_cols(p)], sent.at[1], q2_r.at[p],
            chip(ORDER[p][1], offset(s)),
        )

    def back_opposite(p, i):
        at = chunk_at(p, 0, 3, i) + (t_cols(c, p),)
        return send(
            T.at[at], RB.at[i, :, part_cols(p)], sent.at[1], qo_r.at[ROUTE[i]],
            chip(ORDER[p][1], (1, 3)[ROUTE[i]]),
        )

    def back_first(p, k):
        a, b, cc = own(p)
        at = place(p, (a + k) % 4, b, cc) + (slice(None), t_cols(c, p))
        return send(
            T.at[at], R3.at[k - 1, :, part_cols(p)], sent.at[0], q3_r.at[p],
            chip(ORDER[p][0], k),
        )

    def down(p, g, half):
        at = plane(p, group(p, g)) + (slice(None), slice(None))
        return jnp.dot(
            H[at].reshape(256, HIDDEN), WD[:, d_cols(half, p)], preferred_element_type=F32
        ).reshape(4, 4, 16, K_WIDTH[p])

    def sum_at(p, *at):
        a, b, _ = own(p)
        i = slice(None) if len(at) == 1 else (a + offset(at[1])) % 4
        at = ((b + offset(at[0])) % 4, i)
        return (at if ORDER[p][1] < ORDER[p][0] else at[::-1]) + (slice(None), part_cols(p))

    far_first = (3, 1, 2, 0)

    def for_sibling(*groups):
        for g in groups:
            for p in parts:
                T[plane(p, group(p, g)) + (slice(None), t_cols(1 - c, p))] = down(p, g, 1 - c).astype(BF16)
                pair(p, g, far_first[0]).start()
        for s in far_first[1:]:
            for g in groups:
                for p in parts:
                    pair(p, g, s).start()

    def for_self(p, g, slot):
        SUM[slot, :, :, :, part_cols(p)] = down(p, g, c)

    def add_up(g, slot, s):
        if g in (1, 2) and ROUTE[s] == g - 1:
            arrived(LINE, narrow, op_r.at[s])
        if g == 0:
            if s in (1, 2):
                arrived((0, 0, pl.ds(0, 2)), narrow, qo_r.at[s - 1])
            for d in range(2):
                arrived(LINE, narrow, di_r.at[d, s])
        for p in parts:
            arrived(LINE, part_cols(p), pr_r.at[p, g, s])
            if g == 0 and s in (1, 2):
                for i in range(4):
                    if ROUTE[i] == s - 1:
                        SUM[(slot,) + sum_at(p, s, i)] += RB[i, :, part_cols(p)].astype(F32)
            total = SUM[(slot,) + sum_at(p, s)] + W[landed(p, g, s)].astype(F32)
            if g in (1, 2) and ROUTE[s] == g - 1:
                total = total + RL[s, :, :, part_cols(p)].astype(F32)
            if g == 0:
                for d in range(2):
                    total = total + RD[d, s, :, :, part_cols(p)].astype(F32)
                if s == 0:
                    SUM[(slot,) + sum_at(p, s)] = total
                    continue
            T[line(p, g, s) + (t_cols(c, p),)] = total.astype(BF16)
            if g == 3:
                opposite(p, s).start()
            elif g > 0:
                direct(p, g - 1, s).start()
            elif s < 3:
                back_second(p, s).start()
            else:
                for i in range(4):
                    back_opposite(p, i).start()

    left(CHUNKS3, wide, sent.at[0])
    left(LINES3, wide, sent.at[1])
    left(PLANES3, wide, sent.at[2])
    left((), wide, sent.at[3])
    pl.semaphore_wait(ready, 1)

    def middle(s):
        for i in (0, 1) if ROUTE[s] == 0 else (1, 0):
            add_up(2 - i, i, s)

    for_sibling(3)
    for p in parts:
        for_self(p, 3, 0)
    for s in far_first:
        add_up(3, 0, s)
    for_sibling(2, 1)
    for g in (2, 1):
        for p in parts:
            for_self(p, g, 2 - g)
    for s in (3, 1, 2):
        middle(s)
    for_sibling(0)
    for p in parts:
        for_self(p, 0, 2)
    add_up(0, 2, 3)
    middle(0)
    for s in (1, 2, 0):
        add_up(0, 2, s)

    for p in parts:
        arrived((0, pl.ds(0, 2)), part_cols(p), q2_r.at[p])
        total = SUM[(2,) + sum_at(p, 0)]
        for s in (1, 2):
            total = total + R2[s - 1, :, :, part_cols(p)].astype(F32)
        SUM[(2,) + sum_at(p, 0)] = total
        T[line(p, 0, 0) + (t_cols(c, p),)] = total.astype(BF16)
        for k in steps:
            back_first(p, k).start()
    for p in parts:
        arrived(CHUNKS3, part_cols(p), q3_r.at[p])
        total = SUM[(2,) + sum_at(p, 0, 0)]
        for k in steps:
            total = total + R3[k - 1, :, part_cols(p)].astype(F32)
        FIN[:, part_cols(p)] = total.astype(BF16)
    finish = send(FIN, FR, x_sem.at[2], x_sem.at[3], sibling)
    finish.start()

    def my_rows(v):
        v = v.astype(F32)
        return jnp.where(c == 0, v[0:8], v[8:16]).astype(BF16)

    out[:, pl.ds(pl.multiple_of(c * HALF, 128), HALF)] = my_rows(FIN[...])
    finish.wait_recv()
    out[:, pl.ds(pl.multiple_of((1 - c) * HALF, 128), HALF)] = my_rows(FR[...])

    finish.wait_send()
    left(CHUNKS3, narrow, sent.at[0])
    left(LINES3, narrow, sent.at[1])
    left(PLANES3, narrow, sent.at[2])
    left((), narrow, sent.at[3])


def shards(tok, ids, gv, sg, su, sd, rg, ru, rd):
    def turned(v):
        return jnp.swapaxes(v, -1, -2)

    def blocks(v):
        return turned(v).reshape(1, ROUTED // 16, 16, D)

    arrays = (tok, turned(ids), turned(gv), turned(sg), turned(su), sd, blocks(rg), blocks(ru), rd)
    dma = pltpu.SemaphoreType.DMA
    vmem = pl.BlockSpec(memory_space=pltpu.VMEM)
    hbm = pl.BlockSpec(memory_space=pl.ANY)
    return pl.pallas_call(
        kernel,
        out_shape=jax.ShapeDtypeStruct((8, D), BF16),
        in_specs=[hbm] * 9,
        out_specs=vmem,
        scratch_shapes=[
            pltpu.VMEM((4, 4, 4, 16, 2 * WIDE), BF16),
            pltpu.VMEM(((UP + ROUTED) // 16, 16, D), BF16),
            pltpu.VMEM((SHARED, D), BF16),
            pltpu.VMEM((SHARED, D), BF16),
            pltpu.VMEM((HIDDEN, D), BF16),
            pltpu.VMEM((4, 4, 4, 16, UP + ROUTED), F32),
            pltpu.VMEM((4, 4, 16, SHARED), F32),
            pltpu.VMEM((4, 4, 16, SHARED), F32),
            pltpu.VMEM((4, 4, 4, 16, HIDDEN), BF16),
            pltpu.VMEM((3, 4, 4, 16, HALF), F32),
            pltpu.VMEM((4, 4, 16, HALF), BF16),
            pltpu.VMEM((2, 4, 4, 16, HALF), BF16),
            pltpu.VMEM((2, 4, 16, HALF), BF16),
            pltpu.VMEM((3, 16, HALF), BF16),
            pltpu.VMEM((4, 16, HALF), BF16),
            pltpu.VMEM((8, D), BF16),
            pltpu.VMEM((3, 8), jnp.int32),
            pltpu.VMEM((3, 8), F32),
            pltpu.VMEM((2, 16, WIDE), BF16),
            pltpu.VMEM((16, WIDE), BF16),
            pltpu.VMEM((16, HALF), BF16),
            pltpu.VMEM((16, HALF), BF16),
            dma((6,)), dma((3,)), dma((4,)), dma((4,)),
            dma((3,)), dma((2, 4)), dma((3,)), dma((2,)), dma((2, 3)), dma((4,)), dma((3, 4)),
            dma((3, 4, 4)), dma((4,)), dma((2, 4)), dma((3,)), dma((2,)), dma((3,)),
            pltpu.SemaphoreType.REGULAR,
        ],
        compiler_params=pltpu.CompilerParams(
            collective_id=0, has_side_effects=True, vmem_limit_bytes=62 << 20
        ),
        name="moe_ffn",
    )(*arrays)


def solution(mesh):
    placed = (
        P(("attn", "ffn"), None),
        P(("attn", "ffn"), None),
        P(("attn", "ffn"), None),
        P(None, "ffn"),
        P(None, "ffn"),
        P("ffn", None),
        P("ffn", None, "attn"),
        P("ffn", None, "attn"),
        P("ffn", "attn", None),
    )
    return jax.shard_map(
        shards, mesh=mesh, in_specs=placed, out_specs=P(("attn", "ffn"), None), check_vma=False
    )
```
